128 devices in a mesh: mp: 8 (over z, x_lo), dp: 16 (over x_hi, y, core).
Axes of the slice: x: 4 (x_hi: 2, x_lo: 2; x = x_hi * 2 + x_lo), y: 4, z: 4, core: 2. Of those that a mesh axis runs over, the one named last changes fastest.
Arguments:
- volume: bfloat16 [16, 64, 64, 2048], P('dp', 'mp'), may hold values from -6 to 6
- kernel_a: bfloat16 [3, 3, 3, 32, 64], replicated, may hold values from -0.21875 to 0.21875
- kernel_b: bfloat16 [3, 3, 3, 64, 128], P(None, None, None, 'mp'), may hold values from -0.15625 to 0.15625
- cotangent: bfloat16 [16, 16, 16, 16, 128], P('dp', None, None, None, 'mp'), may hold values from -6 to 6
Outputs:
- features: bfloat16 [16, 16, 16, 16, 128], P('dp', None, None, None, 'mp')
- grad_a: float32 [3, 3, 3, 32, 64], replicated
- grad_b: float32 [3, 3, 3, 64, 128], P(None, None, None, 'mp')
The draws below stay inside these ranges and needn't reach their ends.
All inputs are finite; a program needn't handle non-finite values.
Results may differ from the reference program's by a relative error of at most 0.0049.
Values may be sent and summed in bfloat16 or wider, within the bound.
A program may use at most 192 MiB of HBM per device.

```python
import math
import jax
import jax.numpy as jnp
from jax import lax

C0 = 32
C1 = 64
C2 = 128
GRID = 64
SAMPLES = 16


def block_levels(key, extent, cuts, least, high):
    factor_of = 1.0
    for position, parts in cuts:
        steps = jax.random.uniform(jax.random.fold_in(jax.random.fold_in(key, 6), position), (parts,), jnp.float32, least / len(cuts), high / len(cuts))
        factor_of = factor_of * jnp.repeat(jnp.exp(steps), extent[position] // parts).reshape((-1,) + (1,) * (len(extent) - 1 - position))
    return factor_of


def gaussian(stream_key, dims, spread, bound, pieces=(), dtype=jnp.bfloat16):
    entries = jax.random.normal(stream_key, dims, jnp.float32) * spread
    if len(pieces) > 0:
        entries = block_levels(stream_key, dims, pieces, -0.22, 0.18) * entries
    return jnp.clip(entries, min=-bound, max=bound).astype(dtype)


def setup_inputs(seed: int = 0) -> dict:
    seeds = jax.random.split(jax.random.key(seed), 5)
    volume = gaussian(seeds[0], (SAMPLES, GRID, GRID, GRID * C0), 1.0, 6.0, ((0, 16), (1, 8)))
    kernel_a = gaussian(seeds[1], (3, 3, 3, C0, C1), (27 * C0) ** -0.5, 0.21875)
    kernel_b = gaussian(seeds[2], (3, 3, 3, C1, C2), (27 * C1) ** -0.5, 0.15625, ((3, 8),))
    cotangent = gaussian(seeds[3], (SAMPLES, GRID // 4, GRID // 4, GRID // 4, C2), 1.0, 6.0, ((0, 16), (4, 8)))
    return dict(volume=volume, kernel_a=kernel_a, kernel_b=kernel_b, cotangent=cotangent)


def forward_conv(padded, kernel):
    return lax.conv_general_dilated(padded, kernel, (2, 2, 2), 'VALID', dimension_numbers=('NDHWC', 'DHWIO', 'NDHWC'), precision=lax.Precision.HIGHEST, preferred_element_type=jnp.float32)

def kernel_grad(padded, grads):
    result = lax.conv_general_dilated(padded, grads, (1, 1, 1), 'VALID', rhs_dilation=(2, 2, 2), dimension_numbers=('CDHWN', 'IDHWO', 'NDHWC'), precision=lax.Precision.HIGHEST, preferred_element_type=jnp.float32)
    return jnp.transpose(result, (1, 2, 3, 0, 4))

def input_grad(grads, kernel):
    flipped = kernel[::-1, ::-1, ::-1]
    return lax.conv_general_dilated(grads, flipped, (1, 1, 1), ((1, 2), (1, 2), (1, 2)), lhs_dilation=(2, 2, 2), dimension_numbers=('NDHWC', 'DHWOI', 'NDHWC'), precision=lax.Precision.HIGHEST, preferred_element_type=jnp.float32)

def pad_low(field):
    return jnp.pad(field, ((0, 0), (1, 0), (1, 0), (1, 0), (0, 0)))

def reference(volume, kernel_a, kernel_b, cotangent):
    weights_a = kernel_a.astype(jnp.float32)
    weights_b = kernel_b.astype(jnp.float32)

    def one_sample(carry, items):
        sample, grads = items
        field = sample.astype(jnp.float32).reshape(1, GRID, GRID, GRID, C0)
        padded_x = pad_low(field)
        pre = forward_conv(padded_x, weights_a)
        hidden = lax.optimization_barrier(jnp.where(pre > 0, pre, 0.3 * pre).astype(jnp.bfloat16))
        padded_h = pad_low(hidden.astype(jnp.float32))
        output = forward_conv(padded_h, weights_b).astype(jnp.bfloat16)
        upstream = grads.astype(jnp.float32)[None]
        part_b = kernel_grad(padded_h, upstream)
        back = lax.optimization_barrier(input_grad(upstream, weights_b).astype(jnp.bfloat16))
        delta = lax.optimization_barrier((back.astype(jnp.float32) * jnp.where(pre > 0, 1.0, 0.3)).astype(jnp.bfloat16))
        part_a = kernel_grad(padded_x, delta.astype(jnp.float32))
        return ((carry[0] + part_a, carry[1] + part_b), output[0])
    start = (jnp.zeros((3, 3, 3, C0, C1), jnp.float32), jnp.zeros((3, 3, 3, C1, C2), jnp.float32))
    totals, features = lax.scan(one_sample, start, (volume, cotangent))
    grad_a = totals[0] / math.sqrt(SAMPLES * (GRID // 2) ** 3)
    grad_b = totals[1] / math.sqrt(SAMPLES * (GRID // 4) ** 3)
    return (features, grad_a, grad_b)
```

```python
import functools
import math

import jax
import jax.numpy as jnp
from jax import lax
from jax.experimental import pallas as pl
from jax.experimental.pallas import tpu as pltpu
from jax.sharding import PartitionSpec as P

BF = jnp.bfloat16
F32 = jnp.float32
MESH = pl.DeviceIdType.MESH
SLABS = 8
CORES = 2
GROUP = SLABS * CORES
ROWS_B = 112
ROWS_A = 32


def dot(lhs, rhs):
    return jnp.dot(lhs, rhs, preferred_element_type=F32)


def dot_nt(lhs, rhs):
    return lax.dot_general(lhs, rhs, (((1,), (1,)), ((), ())), preferred_element_type=F32)


def dot_tn(lhs, rhs):
    return lax.dot_general(lhs, rhs, (((0,), (0,)), ((), ())), preferred_element_type=F32)


def later(tiles):
    zero = jnp.zeros((16, tiles.shape[1]), tiles.dtype)
    return jnp.concatenate([zero, tiles[:-16]], axis=0)


def earlier(tiles):
    zero = jnp.zeros((16, tiles.shape[1]), tiles.dtype)
    return jnp.concatenate([tiles[16:], zero], axis=0)


def row_below(tiles):
    rolled = pltpu.roll(tiles.astype(F32), 1, 0)
    row = lax.broadcasted_iota(jnp.int32, tiles.shape, 0)
    return jnp.where(lax.rem(row, 16) == 0, 0.0, rolled).astype(BF)


def body(
    ring,
    scale_a,
    scale_b,
    x,
    ka,
    kb,
    cot,
    feat,
    ga,
    gb,
    xv,
    xs,
    xt,
    wa,
    pf,
    hs,
    ht,
    ct_loc,
    ct_all,
    kb_all,
    kb_f,
    wb,
    vb,
    cs,
    cc,
    ft,
    fr,
    dd,
    gb_f,
    gb_s,
    gb_1,
    gb_2s,
    gb_2,
    gb_3,
    ga_f,
    ga_s,
    ga_1,
    ga_2s,
    ga_2,
    ga_3,
    x_sem,
    xh_send,
    xh_recv,
    hh_send,
    hh_recv,
    ct_send,
    ct_recv,
    kb_send,
    kb_recv,
    ft_send,
    ft_recv,
    b1_send,
    b1_recv,
    b2_send,
    b2_recv,
    b3_send,
    b3_recv,
    a1_send,
    a1_recv,
    a2_send,
    a2_recv,
    a3_send,
    a3_recv,
):
    mp = lax.axis_index("mp")
    dp = lax.axis_index("dp")
    core = lax.rem(dp, CORES)
    rank = lax.div(dp, CORES)
    me = mp * CORES + core

    def in_group(index):
        return {"mp": lax.div(index, CORES), "dp": rank * CORES + lax.rem(index, CORES)}

    def in_slabs(index):
        return {"mp": index, "dp": dp}

    def in_ring(index):
        return {"mp": mp, "dp": index * CORES + core}

    def others(size, mine, act):
        @pl.loop(1, size)
        def _(step):
            act(lax.rem(mine + step, size))

    def remote(src, dst, send, recv, device):
        return pltpu.make_async_remote_copy(
            src_ref=src, dst_ref=dst, send_sem=send, recv_sem=recv, device_id=device, device_id_type=MESH
        )

    barrier = pltpu.get_barrier_semaphore()
    others(GROUP, me, lambda i: pl.semaphore_signal(barrier, inc=1, device_id=in_group(i), device_id_type=MESH))
    others(ring, rank, lambda i: pl.semaphore_signal(barrier, inc=1, device_id=in_ring(i), device_id_type=MESH))

    def plane_copy(plane):
        return pltpu.make_async_copy(x.at[plane], xv.at[plane + 1], x_sem.at[plane])

    @pl.loop(0, 8)
    def _(step):
        plane_copy(7 - step).start()

    eye = (
        lax.broadcasted_iota(jnp.int32, (16, 16), 0) == lax.broadcasted_iota(jnp.int32, (16, 16), 1)
    ).astype(BF)

    @pl.loop(0, 8)
    def _(pair):
        rows = cot[pl.ds(pl.multiple_of(pair * 512, 512), 512), :]
        ct_loc[:, pl.ds(pl.multiple_of(pair * 512, 512), 512)] = dot_nt(eye, rows).astype(BF)

    ct_loc[:, 4096:4352] = jnp.zeros((16, 256), BF)
    kb_all[mp] = jnp.concatenate([kb[...].astype(F32), jnp.zeros((8, 128), F32)], axis=0).astype(BF)

    pl.semaphore_wait(barrier, GROUP - 1 + ring - 1)

    def x_halo():
        return remote(x.at[7], xv.at[0], xh_send, xh_recv, in_slabs(mp + 1))

    def h_halo():
        return remote(hs.at[4, pl.ds(1, 2)], hs.at[0, pl.ds(1, 2)], hh_send, hh_recv, in_slabs(mp + 1))

    def ct_copy(peer, slot):
        src = ct_loc.at[:, pl.ds(pl.multiple_of(peer * 512, 512), 768)]
        return remote(src, ct_all.at[slot], ct_send.at[peer], ct_recv.at[slot], in_slabs(peer))

    def kb_copy(peer, slot):
        return remote(kb_all.at[mp], kb_all.at[slot], kb_send.at[peer], kb_recv.at[slot], in_slabs(peer))

    def ft_copy(peer, slot):
        return remote(ft.at[peer], fr.at[slot], ft_send.at[peer], ft_recv.at[slot], in_slabs(peer))

    def b1_copy(peer, slot):
        return remote(gb_s.at[peer], gb_1.at[slot], b1_send.at[peer], b1_recv.at[slot], in_group(peer))

    def b2_copy(peer, slot):
        return remote(gb_2s, gb_2.at[slot], b2_send.at[peer], b2_recv.at[slot], in_ring(peer))

    def b3_copy(slot):
        return remote(gb_3.at[core], gb_3.at[slot], b3_send, b3_recv, in_group(mp * CORES + 1 - core))

    def a1_copy(peer, slot):
        return remote(ga_s.at[peer], ga_1.at[slot], a1_send.at[peer], a1_recv.at[slot], in_group(peer))

    def a2_copy(peer, slot):
        return remote(ga_2s, ga_2.at[slot], a2_send.at[peer], a2_recv.at[slot], in_ring(peer))

    def a3_copy(peer, slot):
        return remote(ga_3.at[me], ga_3.at[slot], a3_send.at[peer], a3_recv.at[slot], in_group(peer))

    @pl.when(mp < SLABS - 1)
    def _():
        x_halo().start()

    others(SLABS, mp, lambda i: kb_copy(i, mp).start())
    others(SLABS, mp, lambda i: ct_copy(i, mp).start())
    ct_all[mp] = ct_loc[:, pl.ds(pl.multiple_of(mp * 512, 512), 768)]

    @pl.loop(0, 9)
    def _(ab):
        k0 = ka[ab, 0:32, :]
        k1 = ka[ab, 32:64, :]
        k2 = ka[ab, 64:96, :]
        no = jnp.zeros((32, 64), BF)
        wa[ab, 0:32, :] = jnp.concatenate([k1, no, no, no], axis=1)
        wa[ab, 32:64, :] = jnp.concatenate([k2, k0, no, no], axis=1)
        wa[ab, 64:96, :] = jnp.concatenate([no, k1, no, no], axis=1)
        wa[ab, 96:128, :] = jnp.concatenate([no, k2, k0, no], axis=1)

    pick_row = lax.broadcasted_iota(jnp.int32, (80, 64), 0)
    pick_col = lax.broadcasted_iota(jnp.int32, (80, 64), 1)
    pick = (pick_col == 4 * lax.rem(pick_row, 16) + lax.div(pick_row, 16) - 1).astype(BF)

    def prepare(index):
        rows = dot(pick, xv[index]).astype(BF)
        for s in range(5):
            for q in range(16):
                xs[index, s, q * 16 : q * 16 + 16, :] = rows[s * 16 : s * 16 + 16, q * 128 : q * 128 + 128]

    plane_copy(7).wait()
    prepare(8)

    @pl.loop(0, 4)
    def _(step):
        depth = 3 - step
        plane_copy(2 * depth).wait()
        prepare(2 * depth + 1)

        @pl.when(depth > 0)
        def _():
            plane_copy(2 * depth - 1).wait()

        @pl.when(jnp.logical_and(depth == 0, mp > 0))
        def _():
            x_halo().wait_recv()

        @pl.when(jnp.logical_and(depth == 0, mp == 0))
        def _():
            xv[0] = jnp.zeros((64, 2048), BF)

        prepare(2 * depth)
        weights = wa[...].reshape(9 * 128, 256)
        for rh in range(2):
            parts = [xs[2 * depth + a, 2 * rh + b] for a in range(3) for b in range(3)]
            both = dot(jnp.concatenate(parts, axis=1), weights)
            pre = both[:, :128] + later(both[:, 128:])
            pf[depth, rh] = pre
            hidden = jnp.where(pre > 0, pre, 0.3 * pre).astype(BF)
            hs[depth + 1, rh + 1] = hidden
            if rh == 1:
                hs[depth + 1, 0] = row_below(hidden)

        @pl.when(jnp.logical_and(depth == 3, mp < SLABS - 1))
        def _():
            h_halo().start()

    @pl.loop(0, 9)
    def _(index):
        for s in range(5):
            xt[index, s] = xs[index, s].T

    others(SLABS, mp, lambda i: kb_copy(i, i).wait_recv())

    @pl.loop(0, 8)
    def _(e):
        kb_f[e] = kb_all[e].astype(F32)

    @pl.loop(0, 9)
    def _(ab):
        k0, k1, k2 = [
            kb_f[:, pl.ds(pl.multiple_of(ab * 24 + c * 8, 8), 8), :].reshape(64, 128) for c in range(3)
        ]
        this = jnp.concatenate([k1, k2], axis=0)
        last = jnp.concatenate([jnp.zeros((64, 128), F32), k0], axis=0)
        wb[ab] = jnp.concatenate([this, last], axis=1).astype(BF)
        vb[ab] = jnp.concatenate([this.T, last.T], axis=1).astype(BF)

    others(SLABS, mp, lambda i: ct_copy(i, i).wait_recv())
    order_row = lax.broadcasted_iota(jnp.int32, (512, 256), 0)
    order_col = lax.broadcasted_iota(jnp.int32, (512, 256), 1)
    order_pos = lax.rem(order_row, 256)
    order = (
        order_col == (lax.rem(order_pos, 16) + lax.div(order_row, 256)) * 16 + lax.div(order_pos, 16)
    ).astype(BF)
    for p in range(3):
        lanes = ct_all[:, :, p * 256 : p * 256 + 256].reshape(128, 256)
        both = dot_nt(order, lanes).astype(BF)
        cs[p, 0] = both[:256]
        cs[p, 1] = both[256:]
        if p < 2:
            cc[p] = jnp.concatenate([both[:256], earlier(both[:256])], axis=1)

    @pl.when(mp > 0)
    def _():
        h_halo().wait_recv()

    @pl.when(mp == 0)
    def _():
        hs[0] = jnp.zeros((3, 256, 128), BF)

    hs[0, 0] = row_below(hs[0, 2])

    @pl.loop(0, 5)
    def _(index):
        for b in range(3):
            ht[index, b] = hs[index, b].T

    @pl.loop(0, 2)
    def _(depth):
        parts = [hs[2 * depth + a, b] for a in range(3) for b in range(3)]
        both = dot(jnp.concatenate(parts, axis=1), wb[...].reshape(9 * 128, 256))
        out = (both[:, :128] + later(both[:, 128:])).astype(BF)
        turned = dot_tn(out, order[:256]).astype(BF)
        ft[:, :, pl.ds(pl.multiple_of(depth * 256, 256), 256)] = turned.reshape(8, 16, 256)

    others(SLABS, mp, lambda i: ft_copy(i, mp).start())
    fr[mp] = ft[mp]

    @pl.loop(0, 3)
    def _(a):
        lhs = jnp.concatenate(
            [jnp.concatenate([ht[2 * p + a, b] for b in range(3)], axis=0) for p in range(2)], axis=1
        )
        acc = dot(lhs, cc[...].reshape(512, 256))
        for b in range(3):
            block = acc[b * 128 : b * 128 + 128]
            pieces = (block[64:, 128:], block[:64, :128], block[64:, :128])
            for c in range(3):
                start = pl.multiple_of(a * 72 + b * 24 + c * 8, 8)
                gb_f[:, pl.ds(start, 8), :] = pieces[c].reshape(8, 8, 128)

    gb_f[:, 216:224, :] = jnp.zeros((8, 8, 128), F32)

    @pl.loop(0, 8)
    def _(e):
        for k in range(CORES):
            gb_s[e * CORES + k] = gb_f[e, k * ROWS_B : (k + 1) * ROWS_B, :].astype(BF)

    others(GROUP, me, lambda i: b1_copy(i, me).start())
    gb_1[me] = gb_s[me]

    @pl.loop(0, 2)
    def _(depth):
        for rd in range(2):
            for rh in range(2):
                along = [(1, 0)] if rd == 0 else [(2, 0), (0, 1)]
                down = [(1, 0)] if rh == 0 else [(2, 0), (0, 1)]
                lhs = [cs[depth + ahead, low] for _, ahead in along for _, low in down]
                rhs = [vb[a * 3 + b] for a, _ in along for b, _ in down]
                both = dot(jnp.concatenate(lhs, axis=1), jnp.concatenate(rhs, axis=0))
                back = (both[:, :128] + earlier(both[:, 128:])).astype(BF).astype(F32)
                slope = jnp.where(pf[2 * depth + rd, rh] > 0, 1.0, 0.3)
                delta = back * slope
                dd[2 * depth + rd, rh] = jnp.concatenate([delta, earlier(delta)], axis=1).astype(BF)

    others(GROUP, me, lambda i: b1_copy(i, i).wait_recv())
    gb_2s[...] = jnp.sum(gb_1[...].astype(F32), axis=0)
    others(ring, rank, lambda i: b2_copy(i, rank).start())
    gb_2[rank] = gb_2s[...]

    lane = lax.broadcasted_iota(jnp.int32, (16, 128), 1)

    @pl.loop(0, 3)
    def _(a):
        lhs = jnp.concatenate(
            [
                jnp.concatenate([xt[2 * depth + a, 2 * rh + b] for b in range(3)], axis=0)
                for depth in range(4)
                for rh in range(2)
            ],
            axis=1,
        )
        acc = dot(lhs, dd[...].reshape(2048, 256))
        for b in range(3):
            this = acc[b * 128 : b * 128 + 128, :128]
            last = acc[b * 128 + 96 : b * 128 + 128, 128:]
            turned = pltpu.roll(this, 64, 1)
            sums = (last + turned[32:64], this[0:32] + turned[64:96], this[32:64] + turned[96:128])
            for c in range(3):
                packed = jnp.where(lane < 64, sums[c][:16], pltpu.roll(sums[c][16:], 64, 1))
                ga_f[pl.ds(pl.multiple_of(a * 144 + b * 48 + c * 16, 16), 16), :] = packed

    ga_f[432:512, :] = jnp.zeros((80, 128), F32)
    ga_s[...] = ga_f[...].reshape(GROUP, ROWS_A, 128).astype(BF)
    others(GROUP, me, lambda i: a1_copy(i, me).start())
    ga_1[me] = ga_s[me]

    others(ring, rank, lambda i: b2_copy(i, i).wait_recv())
    gb_3[core] = jnp.sum(gb_2[...], axis=0) * scale_b
    b3_copy(core).start()

    others(GROUP, me, lambda i: a1_copy(i, i).wait_recv())
    ga_2s[...] = jnp.sum(ga_1[...].astype(F32), axis=0)
    others(ring, rank, lambda i: a2_copy(i, rank).start())
    ga_2[rank] = ga_2s[...]

    others(SLABS, mp, lambda i: ft_copy(i, i).wait_recv())
    for e in range(SLABS):
        feat[:, e * 512 : e * 512 + 512] = fr[e]

    b3_copy(1 - core).wait_recv()
    gb[0:ROWS_B, :] = gb_3[0]
    gb[ROWS_B:216, :] = gb_3[1, : 216 - ROWS_B, :]

    others(ring, rank, lambda i: a2_copy(i, i).wait_recv())
    ga_3[me] = jnp.sum(ga_2[...], axis=0) * scale_a
    others(GROUP, me, lambda i: a3_copy(i, me).start())

    @pl.when(mp < SLABS - 1)
    def _():
        x_halo().wait_send()
        h_halo().wait_send()

    others(SLABS, mp, lambda i: kb_copy(i, mp).wait_send())
    others(SLABS, mp, lambda i: ct_copy(i, mp).wait_send())
    others(SLABS, mp, lambda i: ft_copy(i, mp).wait_send())
    others(GROUP, me, lambda i: b1_copy(i, me).wait_send())
    others(ring, rank, lambda i: b2_copy(i, rank).wait_send())
    b3_copy(core).wait_send()
    others(GROUP, me, lambda i: a1_copy(i, me).wait_send())
    others(ring, rank, lambda i: a2_copy(i, rank).wait_send())

    others(GROUP, me, lambda i: a3_copy(i, i).wait_recv())
    whole = ga_3[...].reshape(GROUP * ROWS_A, 128)[:432].reshape(27, 16, 128)
    ga[:, 0:16, :] = whole[:, :, :64]
    ga[:, 16:32, :] = whole[:, :, 64:]
    others(GROUP, me, lambda i: a3_copy(i, me).wait_send())


def shards(ring, samples, volume, kernel_a, kernel_b, cotangent):
    scale_a = 1.0 / math.sqrt(samples * 32**3)
    scale_b = 1.0 / math.sqrt(samples * 16**3)
    vmem = pltpu.VMEM
    dma = pltpu.SemaphoreType.DMA
    scratch = [
        vmem((9, 64, 2048), BF),
        vmem((9, 5, 256, 128), BF),
        vmem((9, 5, 128, 256), BF),
        vmem((9, 128, 256), BF),
        vmem((4, 2, 256, 128), F32),
        vmem((5, 3, 256, 128), BF),
        vmem((5, 3, 128, 256), BF),
        vmem((16, 4352), BF),
        vmem((8, 16, 768), BF),
        vmem((8, 224, 128), BF),
        vmem((8, 224, 128), F32),
        vmem((9, 128, 256), BF),
        vmem((9, 128, 256), BF),
        vmem((3, 2, 256, 128), BF),
        vmem((2, 256, 256), BF),
        vmem((8, 16, 512), BF),
        vmem((8, 16, 512), BF),
        vmem((4, 2, 256, 256), BF),
        vmem((8, 224, 128), F32),
        vmem((GROUP, ROWS_B, 128), BF),
        vmem((GROUP, ROWS_B, 128), BF),
        vmem((ROWS_B, 128), F32),
        vmem((ring, ROWS_B, 128), F32),
        vmem((CORES, ROWS_B, 128), F32),
        vmem((512, 128), F32),
        vmem((GROUP, ROWS_A, 128), BF),
        vmem((GROUP, ROWS_A, 128), BF),
        vmem((ROWS_A, 128), F32),
        vmem((ring, ROWS_A, 128), F32),
        vmem((GROUP, ROWS_A, 128), F32),
        dma((8,)),
        dma,
        dma,
        dma,
        dma,
        dma((8,)),
        dma((8,)),
        dma((8,)),
        dma((8,)),
        dma((8,)),
        dma((8,)),
        dma((GROUP,)),
        dma((GROUP,)),
        dma((ring,)),
        dma((ring,)),
        dma,
        dma,
        dma((GROUP,)),
        dma((GROUP,)),
        dma((ring,)),
        dma((ring,)),
        dma((GROUP,)),
        dma((GROUP,)),
    ]
    in_vmem = pl.BlockSpec(memory_space=pltpu.VMEM)
    feat, ga, gb = pl.pallas_call(
        functools.partial(body, ring, scale_a, scale_b),
        out_shape=(
            jax.ShapeDtypeStruct((16, 4096), BF),
            jax.ShapeDtypeStruct((27, 32, 64), F32),
            jax.ShapeDtypeStruct((216, 128), F32),
        ),
        in_specs=[pl.BlockSpec(memory_space=pl.ANY), in_vmem, in_vmem, in_vmem],
        out_specs=(in_vmem, in_vmem, in_vmem),
        scratch_shapes=scratch,
        compiler_params=pltpu.CompilerParams(
            collective_id=0, has_side_effects=True, vmem_limit_bytes=48 * 1024 * 1024
        ),
        cost_estimate=pl.CostEstimate(flops=1600000000, bytes_accessed=4000000, transcendentals=0),
    )(
        volume.reshape(8, 64, 2048),
        kernel_a.reshape(9, 96, 64),
        kernel_b.reshape(216, 128),
        cotangent.reshape(4096, 16),
    )
    features = feat.T.reshape(1, 16, 16, 16, 16)
    return (features, ga.reshape(3, 3, 3, 32, 64), gb.reshape(3, 3, 3, 8, 128))


def solution(mesh):
    ring = mesh.shape["dp"] // CORES
    return jax.shard_map(
        functools.partial(shards, ring, mesh.shape["dp"]),
        mesh=mesh,
        in_specs=(
            P("dp", "mp", None, None),
            P(),
            P(None, None, None, "mp", None),
            P("dp", None, None, None, "mp"),
        ),
        out_specs=(P("dp", None, None, None, "mp"), P(), P(None, None, None, "mp", None)),
        check_vma=False,
    )
```

```python
import functools
import math

import jax
import jax.numpy as jnp
from jax import lax
from jax.experimental import pallas as pl
from jax.experimental.pallas import tpu as pltpu
from jax.sharding import PartitionSpec as P

BF = jnp.bfloat16
F32 = jnp.float32
MESH = pl.DeviceIdType.MESH
SLABS = 8
CORES = 2
GROUP = SLABS * CORES
ROWS_B = 112
ROWS_A = 32


def dot(lhs, rhs):
    return jnp.dot(lhs, rhs, preferred_element_type=F32)


def dot_nt(lhs, rhs):
    return lax.dot_general(lhs, rhs, (((1,), (1,)), ((), ())), preferred_element_type=F32)


def dot_tn(lhs, rhs):
    return lax.dot_general(lhs, rhs, (((0,), (0,)), ((), ())), preferred_element_type=F32)


def later(tiles):
    zero = jnp.zeros((16, tiles.shape[1]), tiles.dtype)
    return jnp.concatenate([zero, tiles[:-16]], axis=0)


def earlier(tiles):
    zero = jnp.zeros((16, tiles.shape[1]), tiles.dtype)
    return jnp.concatenate([tiles[16:], zero], axis=0)


def row_below(tiles):
    rolled = pltpu.roll(tiles.astype(F32), 1, 0)
    row = lax.broadcasted_iota(jnp.int32, tiles.shape, 0)
    return jnp.where(lax.rem(row, 16) == 0, 0.0, rolled).astype(BF)


def body(
    ring,
    scale_a,
    scale_b,
    x,
    ka_hbm,
    kb_hbm,
    cot_hbm,
    feat,
    ga,
    gb,
    feat_v,
    ga_v,
    xv,
    ka,
    kb,
    cot,
    xs,
    xt,
    wa,
    pf,
    hs,
    ht,
    ct_loc,
    ct_all,
    kb_half,
    kb_all,
    kb_f,
    wb,
    vb,
    cs,
    cc,
    ft,
    fr,
    dd,
    gb_f,
    gb_s,
    gb_1,
    gb_2s,
    gb_2,
    ga_f,
    ga_s,
    ga_1,
    ga_2s,
    ga_2,
    ga_3s,
    ga_3r,
    gb_3r,
    x_sem,
    in_sem,
    out_sem,
    xh_send,
    xh_recv,
    ct_send,
    ct_recv,
    kb_send,
    kb_recv,
    kc_send,
    kc_recv,
    ft_send,
    ft_recv,
    b1_send,
    b1_recv,
    b2_send,
    b2_recv,
    b3_send,
    b3_recv,
    a1_send,
    a1_recv,
    a2_send,
    a2_recv,
    a3_send,
    a3_recv,
):
    mp = lax.axis_index("mp")
    dp = lax.axis_index("dp")
    core = lax.rem(dp, CORES)
    rank = lax.div(dp, CORES)
    me = mp * CORES + core

    def in_group(index):
        return {"mp": lax.div(index, CORES), "dp": rank * CORES + lax.rem(index, CORES)}

    def in_slabs(index):
        return {"mp": index, "dp": dp}

    def in_ring(index):
        return {"mp": mp, "dp": index * CORES + core}

    def others(size, mine, act):
        @pl.loop(1, size)
        def _(step):
            act(lax.rem(mine + step, size))

    def remote(src, dst, send, recv, device):
        return pltpu.make_async_remote_copy(
            src_ref=src, dst_ref=dst, send_sem=send, recv_sem=recv, device_id=device, device_id_type=MESH
        )

    barrier = pltpu.get_barrier_semaphore()
    others(GROUP, me, lambda i: pl.semaphore_signal(barrier, inc=1, device_id=in_group(i), device_id_type=MESH))
    others(ring, rank, lambda i: pl.semaphore_signal(barrier, inc=1, device_id=in_ring(i), device_id_type=MESH))

    def plane_copy(plane):
        return pltpu.make_async_copy(x.at[plane], xv.at[plane + 1], x_sem.at[plane])

    in_cot = pltpu.make_async_copy(cot_hbm, cot, in_sem.at[0])
    in_kb = pltpu.make_async_copy(kb_hbm, kb, in_sem.at[1])
    in_ka = pltpu.make_async_copy(ka_hbm, ka, in_sem.at[2])
    in_cot.start()
    in_kb.start()
    in_ka.start()

    @pl.loop(0, 8)
    def _(step):
        plane_copy(7 - step).start()

    in_kb.wait()
    in_ka.wait()
    in_cot.wait()

    eye = (
        lax.broadcasted_iota(jnp.int32, (16, 16), 0) == lax.broadcasted_iota(jnp.int32, (16, 16), 1)
    ).astype(BF)

    @pl.loop(0, 8)
    def _(pair):
        rows = cot[pl.ds(pl.multiple_of(pair * 512, 512), 512), :]
        ct_loc[:, pl.ds(pl.multiple_of(pair * 512, 512), 512)] = dot_nt(eye, rows).astype(BF)

    ct_loc[:, 4096:4352] = jnp.zeros((16, 256), BF)
    share = jnp.concatenate([kb[...].astype(F32), jnp.zeros((8, 128), F32)], axis=0).astype(BF)
    kb_half[0] = share[:ROWS_B]
    kb_half[1] = share[ROWS_B:]
    kb_all[core, mp] = kb_half[core]

    pl.semaphore_wait(barrier, GROUP - 1 + ring - 1)

    def x_halo():
        return remote(x.at[7], xv.at[0], xh_send, xh_recv, in_slabs(mp + 1))

    def ct_copy(peer, slot):
        src = ct_loc.at[:, pl.ds(pl.multiple_of(peer * 512, 512), 768)]
        return remote(src, ct_all.at[slot], ct_send.at[peer], ct_recv.at[slot], in_slabs(peer))

    def kb_copy(peer, slot):
        return remote(
            kb_all.at[core, mp], kb_all.at[core, slot], kb_send.at[peer], kb_recv.at[slot], in_slabs(peer)
        )

    def kc_copy(half):
        return remote(kb_all.at[half], kb_all.at[half], kc_send, kc_recv, in_group(mp * CORES + 1 - core))

    def ft_copy(peer, slot):
        return remote(ft.at[peer], fr.at[slot], ft_send.at[peer], ft_recv.at[slot], in_slabs(peer))

    def b1_copy(peer, slot):
        return remote(gb_s.at[peer], gb_1.at[slot], b1_send.at[peer], b1_recv.at[slot], in_group(peer))

    def b2_copy(peer, slot):
        return remote(gb_2s, gb_2.at[slot], b2_send.at[peer], b2_recv.at[slot], in_ring(peer))

    def b3_copy(slot):
        return remote(gb_3r.at[core], gb_3r.at[slot], b3_send, b3_recv, in_group(mp * CORES + 1 - core))

    def a1_copy(peer, slot):
        return remote(ga_s.at[peer], ga_1.at[slot], a1_send.at[peer], a1_recv.at[slot], in_group(peer))

    def a2_copy(peer, slot):
        return remote(ga_2s, ga_2.at[slot], a2_send.at[peer], a2_recv.at[slot], in_ring(peer))

    def a3_copy(peer, slot):
        return remote(ga_3s, ga_3r.at[slot], a3_send.at[peer], a3_recv.at[slot], in_group(peer))

    @pl.when(mp < SLABS - 1)
    def _():
        x_halo().start()

    others(SLABS, mp, lambda i: ct_copy(i, mp).start())
    others(SLABS, mp, lambda i: kb_copy(i, mp).start())
    ct_all[mp] = ct_loc[:, pl.ds(pl.multiple_of(mp * 512, 512), 768)]

    @pl.loop(0, 9)
    def _(ab):
        k0 = ka[ab, 0:32, :]
        k1 = ka[ab, 32:64, :]
        k2 = ka[ab, 64:96, :]
        no = jnp.zeros((32, 64), BF)
        wa[ab, 0:32, :] = jnp.concatenate([k1, no, no, no], axis=1)
        wa[ab, 32:64, :] = jnp.concatenate([k2, k0, no, no], axis=1)
        wa[ab, 64:96, :] = jnp.concatenate([no, k1, no, no], axis=1)
        wa[ab, 96:128, :] = jnp.concatenate([no, k2, k0, no], axis=1)

    pick_row = lax.broadcasted_iota(jnp.int32, (80, 64), 0)
    pick_col = lax.broadcasted_iota(jnp.int32, (80, 64), 1)
    pick = (pick_col == 4 * lax.rem(pick_row, 16) + lax.div(pick_row, 16) - 1).astype(BF)

    def prepare(index):
        rows = dot(pick, xv[index]).astype(BF)
        for s in range(5):
            for q in range(16):
                xs[index, s, q * 16 : q * 16 + 16, :] = rows[s * 16 : s * 16 + 16, q * 128 : q * 128 + 128]

    def convolve(depth):
        weights = wa[...].reshape(9 * 128, 256)
        for rh in range(2):
            parts = [xs[2 * depth + a, 2 * rh + b] for a in range(3) for b in range(3)]
            both = dot(jnp.concatenate(parts, axis=1), weights)
            pre = both[:, :128] + later(both[:, 128:])
            pf[depth, rh] = pre
            hidden = jnp.where(pre > 0, pre, 0.3 * pre).astype(BF)
            hs[depth, rh + 1] = hidden
            if rh == 1:
                hs[depth, 0] = row_below(hidden)

    plane_copy(7).wait()
    prepare(8)

    @pl.loop(0, 3)
    def _(step):
        depth = 3 - step
        plane_copy(2 * depth).wait()
        prepare(2 * depth + 1)
        plane_copy(2 * depth - 1).wait()
        prepare(2 * depth)
        convolve(depth)

    plane_copy(0).wait()
    prepare(1)

    def turn_x(index):
        for s in range(5):
            xt[index, s] = xs[index, s].T

    def turn_h(index):
        for b in range(3):
            ht[index, b] = hs[index, b].T

    @pl.loop(1, 9)
    def _(index):
        turn_x(index)

    @pl.loop(1, 4)
    def _(index):
        turn_h(index)

    others(SLABS, mp, lambda i: ct_copy(i, i).wait_recv())
    order_row = lax.broadcasted_iota(jnp.int32, (512, 256), 0)
    order_col = lax.broadcasted_iota(jnp.int32, (512, 256), 1)
    order_pos = lax.rem(order_row, 256)
    order = (
        order_col == (lax.rem(order_pos, 16) + lax.div(order_row, 256)) * 16 + lax.div(order_pos, 16)
    ).astype(BF)
    for p in range(3):
        lanes = ct_all[:, :, p * 256 : p * 256 + 256].reshape(128, 256)
        both = dot_nt(order, lanes).astype(BF)
        cs[p, 0] = both[:256]
        cs[p, 1] = both[256:]
        cc[p] = jnp.concatenate([both[:256], earlier(both[:256])], axis=1)

    @pl.when(mp > 0)
    def _():
        x_halo().wait_recv()

    @pl.when(mp == 0)
    def _():
        xv[0] = jnp.zeros((64, 2048), BF)

    prepare(0)
    convolve(0)
    turn_h(0)

    others(SLABS, mp, lambda i: kb_copy(i, i).wait_recv())
    kc_copy(core).start()

    def grad_b_rows(a, planes, cots):
        lhs = jnp.concatenate(
            [jnp.concatenate([ht[plane, b] for b in range(3)], axis=0) for plane in planes], axis=1
        )
        rhs = jnp.concatenate([cc[p] for p in cots], axis=0)
        acc = dot(lhs, rhs)
        for b in range(3):
            block = acc[b * 128 : b * 128 + 128]
            pieces = (block[64:, 128:], block[:64, :128], block[64:, :128])
            for c in range(3):
                start = a * 72 + b * 24 + c * 8
                gb_f[:, start : start + 8, :] = pieces[c].reshape(8, 8, 128)

    grad_b_rows(0, (1, 3), (1, 2))
    grad_b_rows(1, (0, 2), (0, 1))
    grad_b_rows(2, (1, 3), (0, 1))
    gb_f[:, 216:224, :] = jnp.zeros((8, 8, 128), F32)

    @pl.loop(0, 8)
    def _(e):
        for k in range(CORES):
            gb_s[e * CORES + k] = gb_f[e, k * ROWS_B : (k + 1) * ROWS_B, :].astype(BF)

    others(GROUP, me, lambda i: b1_copy(i, me).start())
    gb_1[me] = gb_s[me]
    turn_x(0)

    kc_copy(1 - core).wait_recv()

    @pl.loop(0, 8)
    def _(e):
        kb_f[e, 0:ROWS_B] = kb_all[0, e].astype(F32)
        kb_f[e, ROWS_B : 2 * ROWS_B] = kb_all[1, e].astype(F32)

    @pl.loop(0, 9)
    def _(ab):
        k0, k1, k2 = [
            kb_f[:, pl.ds(pl.multiple_of(ab * 24 + c * 8, 8), 8), :].reshape(64, 128) for c in range(3)
        ]
        this = jnp.concatenate([k1, k2], axis=0)
        last = jnp.concatenate([jnp.zeros((64, 128), F32), k0], axis=0)
        wb[ab] = jnp.concatenate([this, last], axis=1).astype(BF)
        vb[ab] = jnp.concatenate([this.T, last.T], axis=1).astype(BF)

    @pl.loop(0, 2)
    def _(depth):
        for rd in range(2):
            for rh in range(2):
                along = [(1, 0)] if rd == 0 else [(2, 0), (0, 1)]
                down = [(1, 0)] if rh == 0 else [(2, 0), (0, 1)]
                lhs = [cs[depth + ahead, low] for _, ahead in along for _, low in down]
                rhs = [vb[a * 3 + b] for a, _ in along for b, _ in down]
                both = dot(jnp.concatenate(lhs, axis=1), jnp.concatenate(rhs, axis=0))
                back = (both[:, :128] + earlier(both[:, 128:])).astype(BF).astype(F32)
                slope = jnp.where(pf[2 * depth + rd, rh] > 0, 1.0, 0.3)
                delta = back * slope
                dd[2 * depth + rd, rh] = jnp.concatenate([delta, earlier(delta)], axis=1).astype(BF)

    lane = lax.broadcasted_iota(jnp.int32, (16, 128), 1)

    @pl.loop(0, 3)
    def _(a):
        lhs = jnp.concatenate(
            [
                jnp.concatenate([xt[2 * depth + a, 2 * rh + b] for b in range(3)], axis=0)
                for depth in range(4)
                for rh in range(2)
            ],
            axis=1,
        )
        acc = dot(lhs, dd[...].reshape(2048, 256))
        for b in range(3):
            this = acc[b * 128 : b * 128 + 128, :128]
            last = acc[b * 128 + 96 : b * 128 + 128, 128:]
            turned = pltpu.roll(this, 64, 1)
            sums = (last + turned[32:64], this[0:32] + turned[64:96], this[32:64] + turned[96:128])
            for c in range(3):
                packed = jnp.where(lane < 64, sums[c][:16], pltpu.roll(sums[c][16:], 64, 1))
                ga_f[pl.ds(pl.multiple_of(a * 144 + b * 48 + c * 16, 16), 16), :] = packed

    ga_f[432:512, :] = jnp.zeros((80, 128), F32)
    ga_s[...] = ga_f[...].reshape(GROUP, ROWS_A, 128).astype(BF)
    others(GROUP, me, lambda i: a1_copy(i, me).start())
    ga_1[me] = ga_s[me]

    def features_of(plane, terms):
        lhs = [hs[p, b] for p, _ in terms for b in range(3)]
        rhs = [wb[a * 3 + b] for _, a in terms for b in range(3)]
        both = dot(jnp.concatenate(lhs, axis=1), jnp.concatenate(rhs, axis=0))
        out = (both[:, :128] + later(both[:, 128:])).astype(BF)
        turned = dot_tn(out, order[:256]).astype(BF)
        ft[:, :, plane * 256 : plane * 256 + 256] = turned.reshape(8, 16, 256)

    features_of(0, [(0, 1), (1, 2)])
    features_of(1, [(1, 0), (2, 1), (3, 2)])
    features_of(2, [(3, 0)])
    others(SLABS, mp, lambda i: ft_copy(i, mp).start())
    fr[mp] = ft[mp]

    others(GROUP, me, lambda i: b1_copy(i, i).wait_recv())
    gb_2s[...] = jnp.sum(gb_1[...].astype(F32), axis=0).astype(BF)
    others(ring, rank, lambda i: b2_copy(i, rank).start())
    gb_2[rank] = gb_2s[...]

    others(GROUP, me, lambda i: a1_copy(i, i).wait_recv())
    ga_2s[...] = jnp.sum(ga_1[...].astype(F32), axis=0)
    others(ring, rank, lambda i: a2_copy(i, rank).start())
    ga_2[rank] = ga_2s[...]

    others(ring, rank, lambda i: b2_copy(i, i).wait_recv())
    gb_3r[core] = jnp.sum(gb_2[...].astype(F32), axis=0) * scale_b
    b3_copy(core).start()

    others(ring, rank, lambda i: a2_copy(i, i).wait_recv())
    ga_3s[...] = (jnp.sum(ga_2[...], axis=0) * scale_a).astype(BF)
    others(GROUP, me, lambda i: a3_copy(i, me).start())
    ga_3r[me] = ga_3s[...]

    others(SLABS, mp, lambda i: ft_copy(i, i).wait_recv())
    for e in range(SLABS):
        first = fr[e, :, 0:256].astype(F32)
        if e > 0:
            first = first + fr[e - 1, :, 512:768].astype(F32)
        planes = jnp.concatenate([first.astype(BF), fr[e, :, 256:512]], axis=1)
        feat_v[e * 512 : e * 512 + 512, :] = dot_tn(planes, eye).astype(BF)

    out_feat = pltpu.make_async_copy(feat_v, feat, out_sem.at[0])
    out_feat.start()

    @pl.when(mp < SLABS - 1)
    def _():
        x_halo().wait_send()

    others(SLABS, mp, lambda i: kb_copy(i, mp).wait_send())
    kc_copy(core).wait_send()
    others(SLABS, mp, lambda i: ct_copy(i, mp).wait_send())
    others(SLABS, mp, lambda i: ft_copy(i, mp).wait_send())
    others(GROUP, me, lambda i: b1_copy(i, me).wait_send())
    others(ring, rank, lambda i: b2_copy(i, rank).wait_send())
    others(GROUP, me, lambda i: a1_copy(i, me).wait_send())
    others(ring, rank, lambda i: a2_copy(i, rank).wait_send())

    b3_copy(1 - core).wait_recv()
    out_gb = pltpu.make_async_copy(gb_3r, gb, out_sem.at[1])
    out_gb.start()
    b3_copy(core).wait_send()
    others(GROUP, me, lambda i: a3_copy(i, i).wait_recv())
    whole = ga_3r[...].astype(F32).reshape(GROUP * ROWS_A, 128)[:432].reshape(27, 16, 128)
    ga_v[:, 0:16, :] = whole[:, :, :64]
    ga_v[:, 16:32, :] = whole[:, :, 64:]
    out_ga = pltpu.make_async_copy(ga_v, ga, out_sem.at[2])
    out_ga.start()
    others(GROUP, me, lambda i: a3_copy(i, me).wait_send())
    out_feat.wait()
    out_gb.wait()
    out_ga.wait()


def finish(feat_in, ga_in, gb_in, feat, ga, gb, feat_v, ga_v, gb_v, in_sem, out_sem):
    rest = 216 - ROWS_B
    inward = [
        pltpu.make_async_copy(feat_in, feat_v, in_sem.at[0]),
        pltpu.make_async_copy(ga_in, ga_v, in_sem.at[1]),
        pltpu.make_async_copy(gb_in.at[0], gb_v.at[pl.ds(0, ROWS_B)], in_sem.at[2]),
        pltpu.make_async_copy(gb_in.at[1, pl.ds(0, rest)], gb_v.at[pl.ds(ROWS_B, rest)], in_sem.at[3]),
    ]
    outward = [
        pltpu.make_async_copy(feat_v, feat, out_sem.at[0]),
        pltpu.make_async_copy(ga_v, ga, out_sem.at[1]),
        pltpu.make_async_copy(gb_v, gb, out_sem.at[2]),
    ]
    for copy in inward:
        copy.start()
    inward[0].wait()
    outward[0].start()
    inward[1].wait()
    outward[1].start()
    inward[2].wait()
    inward[3].wait()
    outward[2].start()
    for copy in outward:
        copy.wait()


def shards(ring, samples, volume, kernel_a, kernel_b, cotangent):
    scale_a = 1.0 / math.sqrt(samples * 32**3)
    scale_b = 1.0 / math.sqrt(samples * 16**3)
    vmem = pltpu.VMEM
    dma = pltpu.SemaphoreType.DMA
    scratch = [
        vmem((4096, 16), BF),
        vmem((27, 32, 64), F32),
        vmem((9, 64, 2048), BF),
        vmem((9, 96, 64), BF),
        vmem((216, 128), BF),
        vmem((4096, 16), BF),
        vmem((9, 5, 256, 128), BF),
        vmem((9, 5, 128, 256), BF),
        vmem((9, 128, 256), BF),
        vmem((4, 2, 256, 128), F32),
        vmem((4, 3, 256, 128), BF),
        vmem((4, 3, 128, 256), BF),
        vmem((16, 4352), BF),
        vmem((8, 16, 768), BF),
        vmem((CORES, ROWS_B, 128), BF),
        vmem((CORES, 8, ROWS_B, 128), BF),
        vmem((8, 224, 128), F32),
        vmem((9, 128, 256), BF),
        vmem((9, 128, 256), BF),
        vmem((3, 2, 256, 128), BF),
        vmem((3, 256, 256), BF),
        vmem((8, 16, 768), BF),
        vmem((8, 16, 768), BF),
        vmem((4, 2, 256, 256), BF),
        vmem((8, 224, 128), F32),
        vmem((GROUP, ROWS_B, 128), BF),
        vmem((GROUP, ROWS_B, 128), BF),
        vmem((ROWS_B, 128), BF),
        vmem((ring, ROWS_B, 128), BF),
        vmem((512, 128), F32),
        vmem((GROUP, ROWS_A, 128), BF),
        vmem((GROUP, ROWS_A, 128), BF),
        vmem((ROWS_A, 128), F32),
        vmem((ring, ROWS_A, 128), F32),
        vmem((ROWS_A, 128), BF),
        vmem((GROUP, ROWS_A, 128), BF),
        vmem((CORES, ROWS_B, 128), F32),
        dma((8,)),
        dma((3,)),
        dma((3,)),
        dma,
        dma,
        dma((8,)),
        dma((8,)),
        dma((8,)),
        dma((8,)),
        dma,
        dma,
        dma((8,)),
        dma((8,)),
        dma((GROUP,)),
        dma((GROUP,)),
        dma((ring,)),
        dma((ring,)),
        dma,
        dma,
        dma((GROUP,)),
        dma((GROUP,)),
        dma((ring,)),
        dma((ring,)),
        dma((GROUP,)),
        dma((GROUP,)),
    ]
    in_hbm = pl.BlockSpec(memory_space=pltpu.HBM)
    parts = pl.pallas_call(
        functools.partial(body, ring, scale_a, scale_b),
        out_shape=(
            jax.ShapeDtypeStruct((4096, 16), BF),
            jax.ShapeDtypeStruct((27, 32, 64), F32),
            jax.ShapeDtypeStruct((CORES, ROWS_B, 128), F32),
        ),
        in_specs=[in_hbm] * 4,
        out_specs=(in_hbm, in_hbm, in_hbm),
        scratch_shapes=scratch,
        compiler_params=pltpu.CompilerParams(
            collective_id=0, has_side_effects=True, vmem_limit_bytes=60 * 1024 * 1024
        ),
        cost_estimate=pl.CostEstimate(flops=1600000000, bytes_accessed=4000000, transcendentals=0),
    )(
        volume.reshape(8, 64, 2048),
        kernel_a.reshape(9, 96, 64),
        kernel_b.reshape(216, 128),
        cotangent.reshape(4096, 16),
    )
    feat, ga, gb = pl.pallas_call(
        finish,
        out_shape=(
            jax.ShapeDtypeStruct((4096, 16), BF),
            jax.ShapeDtypeStruct((27, 32, 64), F32),
            jax.ShapeDtypeStruct((216, 128), F32),
        ),
        in_specs=[in_hbm] * 3,
        out_specs=(in_hbm, in_hbm, in_hbm),
        scratch_shapes=[
            vmem((4096, 16), BF),
            vmem((27, 32, 64), F32),
            vmem((216, 128), F32),
            dma((4,)),
            dma((3,)),
        ],
        compiler_params=pltpu.CompilerParams(vmem_limit_bytes=60 * 1024 * 1024),
    )(*parts)
    return (
        feat.reshape(1, 16, 16, 16, 16),
        ga.reshape(3, 3, 3, 32, 64),
        gb.reshape(3, 3, 3, 8, 128),
    )


def solution(mesh):
    ring = mesh.shape["dp"] // CORES
    return jax.shard_map(
        functools.partial(shards, ring, mesh.shape["dp"]),
        mesh=mesh,
        in_specs=(
            P("dp", "mp", None, None),
            P(),
            P(None, None, None, "mp", None),
            P("dp", None, None, None, "mp"),
        ),
        out_specs=(P("dp", None, None, None, "mp"), P(), P(None, None, None, "mp", None)),
        check_vma=False,
    )
```

```python
import functools
import math

import jax
import jax.numpy as jnp
from jax import lax
from jax.experimental import pallas as pl
from jax.experimental.pallas import tpu as pltpu
from jax.sharding import PartitionSpec as P

BF = jnp.bfloat16
F32 = jnp.float32
MESH = pl.DeviceIdType.MESH
SLABS = 8
CORES = 2
GROUP = SLABS * CORES
HALF = 112
ROWS_E = 80
ROWS_L = 48
ROWS_A = 32


def dot(lhs, rhs):
    return jnp.dot(lhs, rhs, preferred_element_type=F32)


def dot_nt(lhs, rhs):
    return lax.dot_general(lhs, rhs, (((1,), (1,)), ((), ())), preferred_element_type=F32)


def dot_tn(lhs, rhs):
    return lax.dot_general(lhs, rhs, (((0,), (0,)), ((), ())), preferred_element_type=F32)


def later(tiles):
    zero = jnp.zeros((16, tiles.shape[1]), tiles.dtype)
    return jnp.concatenate([zero, tiles[:-16]], axis=0)


def earlier(tiles):
    zero = jnp.zeros((16, tiles.shape[1]), tiles.dtype)
    return jnp.concatenate([tiles[16:], zero], axis=0)


def row_below(tiles):
    rolled = pltpu.roll(tiles.astype(F32), 1, 0)
    row = lax.broadcasted_iota(jnp.int32, tiles.shape, 0)
    return jnp.where(lax.rem(row, 16) == 0, 0.0, rolled).astype(BF)


def body(
    ring,
    scale_a,
    scale_b,
    x,
    ka_hbm,
    kb_hbm,
    cot_hbm,
    feat,
    ga,
    gbe,
    gbl,
    xv,
    ka,
    kb,
    cot,
    xs,
    xt,
    wa,
    pf,
    hs,
    ht,
    ct_loc,
    ct_all,
    kb_half,
    kb_all,
    kb_f,
    wb,
    vb,
    cs,
    cc,
    ft_up,
    fr_up,
    ft_low,
    fr_low,
    dd,
    bk,
    acc_a,
    ge_f,
    ge_s,
    ge_0,
    ge_h,
    ge_1,
    ge_2s,
    ge_2,
    ge_3,
    gl_f,
    gl_s,
    gl_0,
    gl_h,
    gl_1,
    gl_2s,
    gl_2,
    gl_3,
    ga_f,
    ga_s,
    ga_1,
    ga_2s,
    ga_2,
    ga_3s,
    ga_3,
    x_sem,
    in_sem,
    xh_send,
    xh_recv,
    ct_send,
    ct_recv,
    kb_send,
    kb_recv,
    kc_send,
    kc_recv,
    fu_send,
    fu_recv,
    fl_send,
    fl_recv,
    e0_send,
    e0_recv,
    e1_send,
    e1_recv,
    e2_send,
    e2_recv,
    e3_send,
    e3_recv,
    l0_send,
    l0_recv,
    l1_send,
    l1_recv,
    l2_send,
    l2_recv,
    l3_send,
    l3_recv,
    a1_send,
    a1_recv,
    a2_send,
    a2_recv,
    a3_send,
    a3_recv,
):
    mp = lax.axis_index("mp")
    dp = lax.axis_index("dp")
    core = lax.rem(dp, CORES)
    rank = lax.div(dp, CORES)
    me = mp * CORES + core

    def in_group(index):
        return {"mp": lax.div(index, CORES), "dp": rank * CORES + lax.rem(index, CORES)}

    def in_slabs(index):
        return {"mp": index, "dp": dp}

    def in_ring(index):
        return {"mp": mp, "dp": index * CORES + core}

    def others(size, mine, act):
        @pl.loop(1, size)
        def _(step):
            act(lax.rem(mine + step, size))

    def remote(src, dst, send, recv, device):
        return pltpu.make_async_remote_copy(
            src_ref=src, dst_ref=dst, send_sem=send, recv_sem=recv, device_id=device, device_id_type=MESH
        )

    barrier = pltpu.get_barrier_semaphore()
    others(GROUP, me, lambda i: pl.semaphore_signal(barrier, inc=1, device_id=in_group(i), device_id_type=MESH))
    others(ring, rank, lambda i: pl.semaphore_signal(barrier, inc=1, device_id=in_ring(i), device_id_type=MESH))

    def plane_copy(plane):
        return pltpu.make_async_copy(x.at[plane], xv.at[plane + 1], x_sem.at[plane])

    in_cot = pltpu.make_async_copy(cot_hbm, cot, in_sem.at[0])
    in_kb = pltpu.make_async_copy(kb_hbm, kb, in_sem.at[1])
    in_ka = pltpu.make_async_copy(ka_hbm, ka, in_sem.at[2])
    in_cot.start()
    in_kb.start()
    in_ka.start()

    @pl.loop(0, 8)
    def _(step):
        plane_copy(7 - step).start()

    in_kb.wait()
    in_ka.wait()
    in_cot.wait()

    eye = (
        lax.broadcasted_iota(jnp.int32, (16, 16), 0) == lax.broadcasted_iota(jnp.int32, (16, 16), 1)
    ).astype(BF)

    @pl.loop(0, 8)
    def _(pair):
        rows = cot[pl.ds(pl.multiple_of(pair * 512, 512), 512), :]
        ct_loc[:, pl.ds(pl.multiple_of(pair * 512, 512), 512)] = dot_nt(eye, rows).astype(BF)

    ct_loc[:, 4096:4352] = jnp.zeros((16, 256), BF)
    share = jnp.concatenate([kb[...].astype(F32), jnp.zeros((8, 128), F32)], axis=0).astype(BF)
    kb_half[0] = share[:HALF]
    kb_half[1] = share[HALF:]
    kb_all[core, mp] = kb_half[core]

    @pl.loop(0, 9)
    def _(ab):
        k0 = ka[ab, 0:32, :]
        k1 = ka[ab, 32:64, :]
        k2 = ka[ab, 64:96, :]
        no = jnp.zeros((32, 64), BF)
        wa[ab, 0:32, :] = jnp.concatenate([k1, no, no, no], axis=1)
        wa[ab, 32:64, :] = jnp.concatenate([k2, k0, no, no], axis=1)
        wa[ab, 64:96, :] = jnp.concatenate([no, k1, no, no], axis=1)
        wa[ab, 96:128, :] = jnp.concatenate([no, k2, k0, no], axis=1)

    pick_row = lax.broadcasted_iota(jnp.int32, (80, 64), 0)
    pick_col = lax.broadcasted_iota(jnp.int32, (80, 64), 1)
    pick = (pick_col == 4 * lax.rem(pick_row, 16) + lax.div(pick_row, 16) - 1).astype(BF)

    def prepare(index):
        rows = dot(pick, xv[index]).astype(BF)
        for s in range(5):
            for q in range(16):
                xs[index, s, q * 16 : q * 16 + 16, :] = rows[s * 16 : s * 16 + 16, q * 128 : q * 128 + 128]

    def convolve(depth):
        weights = wa[...].reshape(9 * 128, 256)
        for rh in range(2):
            parts = [xs[2 * depth + a, 2 * rh + b] for a in range(3) for b in range(3)]
            both = dot(jnp.concatenate(parts, axis=1), weights)
            pre = both[:, :128] + later(both[:, 128:])
            pf[depth, rh] = pre
            hidden = jnp.where(pre > 0, pre, 0.3 * pre).astype(BF)
            hs[depth, rh + 1] = hidden
            if rh == 1:
                hs[depth, 0] = row_below(hidden)

    def both_planes(depth):
        plane_copy(2 * depth).wait()
        prepare(2 * depth + 1)
        plane_copy(2 * depth - 1).wait()
        prepare(2 * depth)
        convolve(depth)

    pl.semaphore_wait(barrier, GROUP - 1 + ring - 1)

    def x_halo():
        return remote(x.at[7], xv.at[0], xh_send, xh_recv, in_slabs(mp + 1))

    def ct_copy(peer, slot):
        src = ct_loc.at[:, pl.ds(pl.multiple_of(peer * 512, 512), 768)]
        return remote(src, ct_all.at[slot], ct_send.at[peer], ct_recv.at[slot], in_slabs(peer))

    def kb_copy(peer, slot):
        return remote(
            kb_all.at[core, mp], kb_all.at[core, slot], kb_send.at[peer], kb_recv.at[slot], in_slabs(peer)
        )

    def kc_copy(half):
        return remote(kb_all.at[half], kb_all.at[half], kc_send, kc_recv, in_group(mp * CORES + 1 - core))

    def fu_copy(peer, slot):
        return remote(ft_up.at[peer], fr_up.at[slot], fu_send.at[peer], fu_recv.at[slot], in_slabs(peer))

    def fl_copy(peer, slot):
        return remote(ft_low.at[peer], fr_low.at[slot], fl_send.at[peer], fl_recv.at[slot], in_slabs(peer))

    def e0_copy():
        return remote(ge_s, ge_0, e0_send, e0_recv, in_group(mp * CORES + 1 - core))

    def e1_copy(peer, slot):
        return remote(ge_h.at[peer], ge_1.at[slot], e1_send.at[peer], e1_recv.at[slot], in_slabs(peer))

    def e2_copy(peer, slot):
        return remote(ge_2s, ge_2.at[slot], e2_send.at[peer], e2_recv.at[slot], in_ring(peer))

    def e3_copy(slot):
        return remote(ge_3.at[core], ge_3.at[slot], e3_send, e3_recv, in_group(mp * CORES + 1 - core))

    def l0_copy():
        return remote(gl_s, gl_0, l0_send, l0_recv, in_group(mp * CORES + 1 - core))

    def l1_copy(peer, slot):
        return remote(gl_h.at[peer], gl_1.at[slot], l1_send.at[peer], l1_recv.at[slot], in_slabs(peer))

    def l2_copy(peer, slot):
        return remote(gl_2s, gl_2.at[slot], l2_send.at[peer], l2_recv.at[slot], in_ring(peer))

    def l3_copy(slot):
        return remote(gl_3.at[core], gl_3.at[slot], l3_send, l3_recv, in_group(mp * CORES + 1 - core))

    def a1_copy(peer, slot):
        return remote(ga_s.at[peer], ga_1.at[slot], a1_send.at[peer], a1_recv.at[slot], in_group(peer))

    def a2_copy(peer, slot):
        return remote(ga_2s, ga_2.at[slot], a2_send.at[peer], a2_recv.at[slot], in_ring(peer))

    def a3_copy(peer, slot):
        return remote(ga_3s, ga_3.at[slot], a3_send.at[peer], a3_recv.at[slot], in_group(peer))

    others(SLABS, mp, lambda i: kb_copy(i, mp).start())
    others(SLABS, mp, lambda i: ct_copy(i, mp).start())

    @pl.when(mp < SLABS - 1)
    def _():
        x_halo().start()

    ct_all[mp] = ct_loc[:, pl.ds(pl.multiple_of(mp * 512, 512), 768)]

    plane_copy(7).wait()
    prepare(8)
    both_planes(3)

    @pl.loop(0, 2)
    def _(step):
        both_planes(2 - step)

    plane_copy(0).wait()
    prepare(1)

    def turn_x(index):
        for s in range(5):
            xt[index, s] = xs[index, s].T

    def turn_h(index):
        for b in range(3):
            ht[index, b] = hs[index, b].T

    @pl.loop(1, 9)
    def _(index):
        turn_x(index)

    @pl.loop(1, 4)
    def _(index):
        turn_h(index)

    others(SLABS, mp, lambda i: kb_copy(i, i).wait_recv())
    kc_copy(core).start()

    others(SLABS, mp, lambda i: ct_copy(i, i).wait_recv())
    order_row = lax.broadcasted_iota(jnp.int32, (512, 256), 0)
    order_col = lax.broadcasted_iota(jnp.int32, (512, 256), 1)
    order_pos = lax.rem(order_row, 256)
    order = (
        order_col == (lax.rem(order_pos, 16) + lax.div(order_row, 256)) * 16 + lax.div(order_pos, 16)
    ).astype(BF)
    for p in range(3):
        lanes = ct_all[:, :, p * 256 : p * 256 + 256].reshape(128, 256)
        both = dot_nt(order, lanes).astype(BF)
        cs[p, 0] = both[:256]
        cs[p, 1] = both[256:]
        cc[p] = jnp.concatenate([both[:256], earlier(both[:256])], axis=1)

    def grad_b_rows(into, first, planes, cots):
        lhs = jnp.concatenate(
            [jnp.concatenate([ht[plane, b] for b in range(3)], axis=0) for plane in planes], axis=1
        )
        rhs = jnp.concatenate([cc[p] for p in cots], axis=0)
        acc = dot(lhs, rhs)
        for b in range(3):
            block = acc[b * 128 : b * 128 + 128]
            pieces = (block[64:, 128:], block[:64, :128], block[64:, :128])
            for c in range(3):
                start = first + b * 24 + c * 8
                into[:, start : start + 8, :] = pieces[c].reshape(8, 8, 128)

    grad_b_rows(ge_f, 0, (1, 3), (1, 2))
    grad_b_rows(ge_f, 72, (1, 3), (0, 1))
    ge_f[:, 144:160, :] = jnp.zeros((8, 16, 128), F32)

    def halves(full, size, other):
        theirs = pl.ds(pl.multiple_of((1 - core) * size, 8), size)
        other[...] = full[:, theirs, :].astype(BF)

    def join(full, size, came, mine):
        own = pl.ds(pl.multiple_of(core * size, 8), size)
        mine[...] = (full[:, own, :] + came[...].astype(F32)).astype(BF)

    halves(ge_f, ROWS_E, ge_s)
    e0_copy().start()

    kc_copy(1 - core).wait_recv()

    @pl.loop(0, 8)
    def _(e):
        kb_f[e, 0:HALF] = kb_all[0, e].astype(F32)
        kb_f[e, HALF : 2 * HALF] = kb_all[1, e].astype(F32)

    @pl.loop(0, 9)
    def _(ab):
        k0, k1, k2 = [
            kb_f[:, pl.ds(pl.multiple_of(ab * 24 + c * 8, 8), 8), :].reshape(64, 128) for c in range(3)
        ]
        this = jnp.concatenate([k1, k2], axis=0)
        last = jnp.concatenate([jnp.zeros((64, 128), F32), k0], axis=0)
        wb[ab] = jnp.concatenate([this, last], axis=1).astype(BF)
        vb[ab] = jnp.concatenate([this.T, last.T], axis=1).astype(BF)

    e0_copy().wait_recv()
    join(ge_f, ROWS_E, ge_0, ge_h)
    others(SLABS, mp, lambda i: e1_copy(i, mp).start())
    ge_1[mp] = ge_h[mp]

    def slope(depth, rh, back):
        delta = back * jnp.where(pf[depth, rh] > 0, 1.0, 0.3)
        dd[depth, rh] = jnp.concatenate([delta, earlier(delta)], axis=1).astype(BF)

    for depth in range(2):
        for rd in range(2):
            for rh in range(2):
                along = [(1, 0)] if rd == 0 else [(2, 0), (0, 1)]
                down = [(1, 0)] if rh == 0 else [(2, 0), (0, 1)]
                lhs = [cs[depth + ahead, low] for _, ahead in along for _, low in down]
                rhs = [vb[a * 3 + b] for a, _ in along for b, _ in down]
                both = dot(jnp.concatenate(lhs, axis=1), jnp.concatenate(rhs, axis=0))
                back = (both[:, :128] + earlier(both[:, 128:])).astype(BF).astype(F32)
                if depth == 0 and rd == 0:
                    bk[rh] = back
                else:
                    slope(2 * depth + rd, rh, back)

    def grad_a_dot(a, depths):
        lhs = jnp.concatenate(
            [
                jnp.concatenate([xt[2 * depth + a, 2 * rh + b] for b in range(3)], axis=0)
                for depth in depths
                for rh in range(2)
            ],
            axis=1,
        )
        rhs = dd[depths[0] : depths[-1] + 1].reshape(512 * len(depths), 256)
        return dot(lhs, rhs)

    @pl.loop(0, 3)
    def _(a):
        acc_a[a] = grad_a_dot(a, (1, 2, 3))

    @pl.when(mp > 0)
    def _():
        x_halo().wait_recv()

    @pl.when(mp == 0)
    def _():
        xv[0] = jnp.zeros((64, 2048), BF)

    prepare(0)
    convolve(0)
    turn_x(0)
    for rh in range(2):
        slope(0, rh, bk[rh])

    lane = lax.broadcasted_iota(jnp.int32, (16, 128), 1)

    @pl.loop(0, 3)
    def _(a):
        acc = acc_a[a] + grad_a_dot(a, (0,))
        for b in range(3):
            this = acc[b * 128 : b * 128 + 128, :128]
            last = acc[b * 128 + 96 : b * 128 + 128, 128:]
            turned = pltpu.roll(this, 64, 1)
            sums = (last + turned[32:64], this[0:32] + turned[64:96], this[32:64] + turned[96:128])
            for c in range(3):
                packed = jnp.where(lane < 64, sums[c][:16], pltpu.roll(sums[c][16:], 64, 1))
                ga_f[pl.ds(pl.multiple_of(a * 144 + b * 48 + c * 16, 16), 16), :] = packed

    ga_f[432:512, :] = jnp.zeros((80, 128), F32)
    ga_s[...] = ga_f[...].reshape(GROUP, ROWS_A, 128).astype(BF)
    others(GROUP, me, lambda i: a1_copy(i, me).start())
    ga_1[me] = ga_s[me]

    turn_h(0)
    grad_b_rows(gl_f, 0, (0, 2), (0, 1))
    gl_f[:, 72:96, :] = jnp.zeros((8, 24, 128), F32)
    halves(gl_f, ROWS_L, gl_s)
    l0_copy().start()
    def features_of(into, place, terms):
        lhs = [hs[p, b] for p, _ in terms for b in range(3)]
        rhs = [wb[a * 3 + b] for _, a in terms for b in range(3)]
        both = dot(jnp.concatenate(lhs, axis=1), jnp.concatenate(rhs, axis=0))
        out = (both[:, :128] + later(both[:, 128:])).astype(BF)
        turned = dot_tn(out, order[:256]).astype(BF)
        into[:, :, place : place + 256] = turned.reshape(8, 16, 256)

    features_of(ft_up, 0, [(1, 0), (2, 1), (3, 2)])
    features_of(ft_up, 256, [(3, 0)])
    others(SLABS, mp, lambda i: fu_copy(i, mp).start())
    fr_up[mp] = ft_up[mp]
    features_of(ft_low, 0, [(0, 1), (1, 2)])
    others(SLABS, mp, lambda i: fl_copy(i, mp).start())
    fr_low[mp] = ft_low[mp]
    others(SLABS, mp, lambda i: e1_copy(i, i).wait_recv())
    ge_2s[...] = jnp.sum(ge_1[...].astype(F32), axis=0).astype(BF)
    others(ring, rank, lambda i: e2_copy(i, rank).start())
    ge_2[rank] = ge_2s[...]
    l0_copy().wait_recv()
    join(gl_f, ROWS_L, gl_0, gl_h)
    others(SLABS, mp, lambda i: l1_copy(i, mp).start())
    gl_1[mp] = gl_h[mp]

    others(GROUP, me, lambda i: a1_copy(i, i).wait_recv())
    ga_2s[...] = jnp.sum(ga_1[...].astype(F32), axis=0)
    others(ring, rank, lambda i: a2_copy(i, rank).start())
    ga_2[rank] = ga_2s[...]

    others(ring, rank, lambda i: e2_copy(i, i).wait_recv())
    ge_3[core] = jnp.sum(ge_2[...].astype(F32), axis=0) * scale_b
    e3_copy(core).start()

    others(SLABS, mp, lambda i: l1_copy(i, i).wait_recv())
    gl_2s[...] = jnp.sum(gl_1[...].astype(F32), axis=0).astype(BF)
    others(ring, rank, lambda i: l2_copy(i, rank).start())
    gl_2[rank] = gl_2s[...]

    others(ring, rank, lambda i: a2_copy(i, i).wait_recv())
    ga_3s[...] = (jnp.sum(ga_2[...], axis=0) * scale_a).astype(BF)
    others(GROUP, me, lambda i: a3_copy(i, me).start())
    ga_3[me] = ga_3s[...]

    others(SLABS, mp, lambda i: fu_copy(i, i).wait_recv())
    others(SLABS, mp, lambda i: fl_copy(i, i).wait_recv())
    for e in range(SLABS):
        first = fr_low[e].astype(F32)
        if e > 0:
            first = first + fr_up[e - 1, :, 256:512].astype(F32)
        planes = jnp.concatenate([first.astype(BF), fr_up[e, :, 0:256]], axis=1)
        feat[e * 512 : e * 512 + 512, :] = dot_tn(planes, eye).astype(BF)

    e3_copy(1 - core).wait_recv()
    gbe[...] = ge_3[...]
    others(ring, rank, lambda i: l2_copy(i, i).wait_recv())
    gl_3[core] = jnp.sum(gl_2[...].astype(F32), axis=0) * scale_b
    l3_copy(core).start()

    @pl.when(mp < SLABS - 1)
    def _():
        x_halo().wait_send()

    others(SLABS, mp, lambda i: kb_copy(i, mp).wait_send())
    kc_copy(core).wait_send()
    others(SLABS, mp, lambda i: ct_copy(i, mp).wait_send())
    others(SLABS, mp, lambda i: fu_copy(i, mp).wait_send())
    others(SLABS, mp, lambda i: fl_copy(i, mp).wait_send())
    e0_copy().wait_send()
    l0_copy().wait_send()
    others(SLABS, mp, lambda i: e1_copy(i, mp).wait_send())
    others(SLABS, mp, lambda i: l1_copy(i, mp).wait_send())
    others(ring, rank, lambda i: e2_copy(i, rank).wait_send())
    e3_copy(core).wait_send()
    others(ring, rank, lambda i: l2_copy(i, rank).wait_send())
    others(GROUP, me, lambda i: a1_copy(i, me).wait_send())
    others(ring, rank, lambda i: a2_copy(i, rank).wait_send())

    l3_copy(1 - core).wait_recv()
    gbl[...] = gl_3[...]
    l3_copy(core).wait_send()
    others(GROUP, me, lambda i: a3_copy(i, i).wait_recv())
    ga[...] = ga_3[...]
    others(GROUP, me, lambda i: a3_copy(i, me).wait_send())


def finish(feat_in, ga_in, gbe, gbl, feat, ga, gb, ga_v, sem):
    moves = [
        (feat_in, feat),
        (gbe.at[0, pl.ds(0, 72)], gb.at[pl.ds(0, 72)]),
        (gbl.at[0, pl.ds(0, 48)], gb.at[pl.ds(72, 48)]),
        (gbl.at[1, pl.ds(0, 24)], gb.at[pl.ds(120, 24)]),
        (gbe.at[0, pl.ds(72, 8)], gb.at[pl.ds(144, 8)]),
        (gbe.at[1, pl.ds(0, 64)], gb.at[pl.ds(152, 64)]),
        (ga_v, ga),
    ]
    copies = [pltpu.make_async_copy(src, dst, sem.at[place]) for place, (src, dst) in enumerate(moves)]
    for copy in copies[:-1]:
        copy.start()
    whole = ga_in[...].astype(F32).reshape(GROUP * ROWS_A, 128)[:432].reshape(27, 16, 128)
    ga_v[:, 0:16, :] = whole[:, :, :64]
    ga_v[:, 16:32, :] = whole[:, :, 64:]
    copies[-1].start()
    for copy in copies:
        copy.wait()


def hbm(array):
    return pltpu.with_memory_space_constraint(array, pltpu.HBM)


def shards(ring, samples, volume, kernel_a, kernel_b, cotangent):
    scale_a = 1.0 / math.sqrt(samples * 32**3)
    scale_b = 1.0 / math.sqrt(samples * 16**3)
    vmem = pltpu.VMEM
    dma = pltpu.SemaphoreType.DMA
    scratch = [
        vmem((9, 64, 2048), BF),
        vmem((9, 96, 64), BF),
        vmem((216, 128), BF),
        vmem((4096, 16), BF),
        vmem((9, 5, 256, 128), BF),
        vmem((9, 5, 128, 256), BF),
        vmem((9, 128, 256), BF),
        vmem((4, 2, 256, 128), F32),
        vmem((4, 3, 256, 128), BF),
        vmem((4, 3, 128, 256), BF),
        vmem((16, 4352), BF),
        vmem((8, 16, 768), BF),
        vmem((CORES, HALF, 128), BF),
        vmem((CORES, 8, HALF, 128), BF),
        vmem((8, 224, 128), F32),
        vmem((9, 128, 256), BF),
        vmem((9, 128, 256), BF),
        vmem((3, 2, 256, 128), BF),
        vmem((3, 256, 256), BF),
        vmem((8, 16, 512), BF),
        vmem((8, 16, 512), BF),
        vmem((8, 16, 256), BF),
        vmem((8, 16, 256), BF),
        vmem((4, 2, 256, 256), BF),
        vmem((2, 256, 128), F32),
        vmem((3, 384, 256), F32),
        vmem((8, 160, 128), F32),
        vmem((8, ROWS_E, 128), BF),
        vmem((8, ROWS_E, 128), BF),
        vmem((8, ROWS_E, 128), BF),
        vmem((8, ROWS_E, 128), BF),
        vmem((ROWS_E, 128), BF),
        vmem((ring, ROWS_E, 128), BF),
        vmem((CORES, ROWS_E, 128), F32),
        vmem((8, 96, 128), F32),
        vmem((8, ROWS_L, 128), BF),
        vmem((8, ROWS_L, 128), BF),
        vmem((8, ROWS_L, 128), BF),
        vmem((8, ROWS_L, 128), BF),
        vmem((ROWS_L, 128), BF),
        vmem((ring, ROWS_L, 128), BF),
        vmem((CORES, ROWS_L, 128), F32),
        vmem((512, 128), F32),
        vmem((GROUP, ROWS_A, 128), BF),
        vmem((GROUP, ROWS_A, 128), BF),
        vmem((ROWS_A, 128), F32),
        vmem((ring, ROWS_A, 128), F32),
        vmem((ROWS_A, 128), BF),
        vmem((GROUP, ROWS_A, 128), BF),
        dma((8,)),
        dma((3,)),
        dma,
        dma,
        dma((8,)),
        dma((8,)),
        dma((8,)),
        dma((8,)),
        dma,
        dma,
        dma((8,)),
        dma((8,)),
        dma((8,)),
        dma((8,)),
        dma,
        dma,
        dma((8,)),
        dma((8,)),
        dma((ring,)),
        dma((ring,)),
        dma,
        dma,
        dma,
        dma,
        dma((8,)),
        dma((8,)),
        dma((ring,)),
        dma((ring,)),
        dma,
        dma,
        dma((GROUP,)),
        dma((GROUP,)),
        dma((ring,)),
        dma((ring,)),
        dma((GROUP,)),
        dma((GROUP,)),
    ]
    in_vmem = pl.BlockSpec(memory_space=pltpu.VMEM)
    in_hbm = pl.BlockSpec(memory_space=pltpu.HBM)
    parts = pl.pallas_call(
        functools.partial(body, ring, scale_a, scale_b),
        out_shape=(
            jax.ShapeDtypeStruct((4096, 16), BF),
            jax.ShapeDtypeStruct((GROUP, ROWS_A, 128), BF),
            jax.ShapeDtypeStruct((CORES, ROWS_E, 128), F32),
            jax.ShapeDtypeStruct((CORES, ROWS_L, 128), F32),
        ),
        in_specs=[in_hbm] * 4,
        out_specs=(in_vmem,) * 4,
        scratch_shapes=scratch,
        compiler_params=pltpu.CompilerParams(
            collective_id=0, has_side_effects=True, vmem_limit_bytes=48 * 1024 * 1024
        ),
        cost_estimate=pl.CostEstimate(flops=1600000000, bytes_accessed=4000000, transcendentals=0),
    )(
        hbm(volume.reshape(8, 64, 2048)),
        hbm(kernel_a.reshape(9, 96, 64)),
        hbm(kernel_b.reshape(216, 128)),
        hbm(cotangent.reshape(4096, 16)),
    )
    feat, ga, gb = pl.pallas_call(
        finish,
        out_shape=(
            jax.ShapeDtypeStruct((4096, 16), BF),
            jax.ShapeDtypeStruct((27, 32, 64), F32),
            jax.ShapeDtypeStruct((216, 128), F32),
        ),
        in_specs=[in_vmem] * 4,
        out_specs=(in_hbm, in_hbm, in_hbm),
        scratch_shapes=[vmem((27, 32, 64), F32), dma((7,))],
        compiler_params=pltpu.CompilerParams(vmem_limit_bytes=4 * 1024 * 1024),
    )(*parts)
    return (
        feat.reshape(1, 16, 16, 16, 16),
        ga.reshape(3, 3, 3, 32, 64),
        gb.reshape(3, 3, 3, 8, 128),
    )


def solution(mesh):
    ring = mesh.shape["dp"] // CORES
    return jax.shard_map(
        functools.partial(shards, ring, mesh.shape["dp"]),
        mesh=mesh,
        in_specs=(
            P("dp", "mp", None, None),
            P(),
            P(None, None, None, "mp", None),
            P("dp", None, None, None, "mp"),
        ),
        out_specs=(P("dp", None, None, None, "mp"), P(), P(None, None, None, "mp", None)),
        check_vma=False,
    )
```

```python
import functools
import math

import jax
import jax.numpy as jnp
from jax import lax
from jax.experimental import pallas as pl
from jax.experimental.pallas import tpu as pltpu
from jax.sharding import PartitionSpec as P

BF = jnp.bfloat16
F32 = jnp.float32
MESH = pl.DeviceIdType.MESH
SLABS = 8
CORES = 2
GROUP = SLABS * CORES
HALF = 112
ROWS_A = 32


def dot(lhs, rhs):
    return jnp.dot(lhs, rhs, preferred_element_type=F32)


def dot_nt(lhs, rhs):
    return lax.dot_general(lhs, rhs, (((1,), (1,)), ((), ())), preferred_element_type=F32)


def dot_tn(lhs, rhs):
    return lax.dot_general(lhs, rhs, (((0,), (0,)), ((), ())), preferred_element_type=F32)


def later(tiles):
    zero = jnp.zeros((16, tiles.shape[1]), tiles.dtype)
    return jnp.concatenate([zero, tiles[:-16]], axis=0)


def earlier(tiles):
    zero = jnp.zeros((16, tiles.shape[1]), tiles.dtype)
    return jnp.concatenate([tiles[16:], zero], axis=0)


def row_below(tiles):
    rolled = pltpu.roll(tiles.astype(F32), 1, 0)
    row = lax.broadcasted_iota(jnp.int32, tiles.shape, 0)
    return jnp.where(lax.rem(row, 16) == 0, 0.0, rolled).astype(BF)


def body(
    ring,
    scale_a,
    scale_b,
    x,
    ka_hbm,
    kb_hbm,
    cot_hbm,
    feat,
    ga,
    gb,
    xv,
    ka,
    kb,
    cot,
    xs,
    xt,
    wa,
    pf,
    hs,
    ht,
    ct_loc,
    ct_all,
    kb_half,
    kb_all,
    kb_f,
    wb,
    vb,
    cs,
    cc,
    ft,
    fr,
    dd,
    bk,
    acc_a,
    gb_f,
    gb_s,
    gb_0,
    gb_h,
    gb_1,
    gb_2s,
    gb_2,
    gb_3,
    ga_f,
    ga_s,
    ga_1,
    ga_2s,
    ga_2,
    ga_3s,
    ga_3,
    x_sem,
    in_sem,
    xh_send,
    xh_recv,
    ct_send,
    ct_recv,
    kb_send,
    kb_recv,
    kc_send,
    kc_recv,
    ft_send,
    ft_recv,
    b0_send,
    b0_recv,
    b1_send,
    b1_recv,
    b2_send,
    b2_recv,
    b3_send,
    b3_recv,
    a1_send,
    a1_recv,
    a2_send,
    a2_recv,
    a3_send,
    a3_recv,
):
    mp = lax.axis_index("mp")
    dp = lax.axis_index("dp")
    core = lax.rem(dp, CORES)
    rank = lax.div(dp, CORES)
    me = mp * CORES + core

    def in_group(index):
        return {"mp": lax.div(index, CORES), "dp": rank * CORES + lax.rem(index, CORES)}

    def in_slabs(index):
        return {"mp": index, "dp": dp}

    def in_ring(index):
        return {"mp": mp, "dp": index * CORES + core}

    def others(size, mine, act):
        @pl.loop(1, size)
        def _(step):
            act(lax.rem(mine + step, size))

    def remote(src, dst, send, recv, device):
        return pltpu.make_async_remote_copy(
            src_ref=src, dst_ref=dst, send_sem=send, recv_sem=recv, device_id=device, device_id_type=MESH
        )

    barrier = pltpu.get_barrier_semaphore()
    others(GROUP, me, lambda i: pl.semaphore_signal(barrier, inc=1, device_id=in_group(i), device_id_type=MESH))
    others(ring, rank, lambda i: pl.semaphore_signal(barrier, inc=1, device_id=in_ring(i), device_id_type=MESH))

    def plane_copy(plane):
        return pltpu.make_async_copy(x.at[plane], xv.at[plane + 1], x_sem.at[plane])

    in_cot = pltpu.make_async_copy(cot_hbm, cot, in_sem.at[0])
    in_kb = pltpu.make_async_copy(kb_hbm, kb, in_sem.at[1])
    in_ka = pltpu.make_async_copy(ka_hbm, ka, in_sem.at[2])
    in_cot.start()
    in_kb.start()
    in_ka.start()

    @pl.loop(0, 8)
    def _(step):
        plane_copy(7 - step).start()

    in_kb.wait()
    in_ka.wait()
    in_cot.wait()

    eye = (
        lax.broadcasted_iota(jnp.int32, (16, 16), 0) == lax.broadcasted_iota(jnp.int32, (16, 16), 1)
    ).astype(BF)

    @pl.loop(0, 8)
    def _(pair):
        rows = cot[pl.ds(pl.multiple_of(pair * 512, 512), 512), :]
        ct_loc[:, pl.ds(pl.multiple_of(pair * 512, 512), 512)] = dot_nt(eye, rows).astype(BF)

    ct_loc[:, 4096:4352] = jnp.zeros((16, 256), BF)
    share = jnp.concatenate([kb[...].astype(F32), jnp.zeros((8, 128), F32)], axis=0).astype(BF)
    kb_half[0] = share[:HALF]
    kb_half[1] = share[HALF:]
    kb_all[core, mp] = kb_half[core]

    @pl.loop(0, 9)
    def _(ab):
        k0 = ka[ab, 0:32, :]
        k1 = ka[ab, 32:64, :]
        k2 = ka[ab, 64:96, :]
        no = jnp.zeros((32, 64), BF)
        wa[ab, 0:32, :] = jnp.concatenate([k1, no, no, no], axis=1)
        wa[ab, 32:64, :] = jnp.concatenate([k2, k0, no, no], axis=1)
        wa[ab, 64:96, :] = jnp.concatenate([no, k1, no, no], axis=1)
        wa[ab, 96:128, :] = jnp.concatenate([no, k2, k0, no], axis=1)

    pick_row = lax.broadcasted_iota(jnp.int32, (80, 64), 0)
    pick_col = lax.broadcasted_iota(jnp.int32, (80, 64), 1)
    pick = (pick_col == 4 * lax.rem(pick_row, 16) + lax.div(pick_row, 16) - 1).astype(BF)

    def prepare(index):
        rows = dot(pick, xv[index]).astype(BF)
        for s in range(5):
            for q in range(16):
                xs[index, s, q * 16 : q * 16 + 16, :] = rows[s * 16 : s * 16 + 16, q * 128 : q * 128 + 128]

    def convolve(depth):
        weights = wa[...].reshape(9 * 128, 256)
        for rh in range(2):
            parts = [xs[2 * depth + a, 2 * rh + b] for a in range(3) for b in range(3)]
            both = dot(jnp.concatenate(parts, axis=1), weights)
            pre = both[:, :128] + later(both[:, 128:])
            pf[depth, rh] = pre
            hidden = jnp.where(pre > 0, pre, 0.3 * pre).astype(BF)
            hs[depth, rh + 1] = hidden
            if rh == 1:
                hs[depth, 0] = row_below(hidden)

    def both_planes(depth):
        plane_copy(2 * depth).wait()
        prepare(2 * depth + 1)
        plane_copy(2 * depth - 1).wait()
        prepare(2 * depth)
        convolve(depth)

    pl.semaphore_wait(barrier, GROUP - 1 + ring - 1)

    def x_halo():
        return remote(x.at[7], xv.at[0], xh_send, xh_recv, in_slabs(mp + 1))

    def ct_copy(peer, slot):
        src = ct_loc.at[:, pl.ds(pl.multiple_of(peer * 512, 512), 768)]
        return remote(src, ct_all.at[slot], ct_send.at[peer], ct_recv.at[slot], in_slabs(peer))

    def kb_copy(peer, slot):
        return remote(
            kb_all.at[core, mp], kb_all.at[core, slot], kb_send.at[peer], kb_recv.at[slot], in_slabs(peer)
        )

    def kc_copy(half):
        return remote(kb_all.at[half], kb_all.at[half], kc_send, kc_recv, in_group(mp * CORES + 1 - core))

    def ft_copy(peer, slot):
        return remote(ft.at[peer], fr.at[slot], ft_send.at[peer], ft_recv.at[slot], in_slabs(peer))

    def b0_copy():
        return remote(gb_s, gb_0, b0_send, b0_recv, in_group(mp * CORES + 1 - core))

    def b1_copy(peer, slot):
        return remote(gb_h.at[peer], gb_1.at[slot], b1_send.at[peer], b1_recv.at[slot], in_slabs(peer))

    def b2_copy(peer, slot):
        return remote(gb_2s, gb_2.at[slot], b2_send.at[peer], b2_recv.at[slot], in_ring(peer))

    def b3_copy(slot):
        return remote(gb_3.at[core], gb_3.at[slot], b3_send, b3_recv, in_group(mp * CORES + 1 - core))

    def a1_copy(peer, slot):
        return remote(ga_s.at[peer], ga_1.at[slot], a1_send.at[peer], a1_recv.at[slot], in_group(peer))

    def a2_copy(peer, slot):
        return remote(ga_2s, ga_2.at[slot], a2_send.at[peer], a2_recv.at[slot], in_ring(peer))

    def a3_copy(peer, slot):
        return remote(ga_3s, ga_3.at[slot], a3_send.at[peer], a3_recv.at[slot], in_group(peer))

    others(SLABS, mp, lambda i: kb_copy(i, mp).start())
    others(SLABS, mp, lambda i: ct_copy(i, mp).start())

    @pl.when(mp < SLABS - 1)
    def _():
        x_halo().start()

    ct_all[mp] = ct_loc[:, pl.ds(pl.multiple_of(mp * 512, 512), 768)]

    plane_copy(7).wait()
    prepare(8)
    both_planes(3)

    @pl.loop(0, 2)
    def _(step):
        both_planes(2 - step)

    plane_copy(0).wait()
    prepare(1)

    def turn_x(index):
        for s in range(5):
            xt[index, s] = xs[index, s].T

    def turn_h(index):
        for b in range(3):
            ht[index, b] = hs[index, b].T

    @pl.loop(1, 9)
    def _(index):
        turn_x(index)

    others(SLABS, mp, lambda i: kb_copy(i, i).wait_recv())
    kc_copy(core).start()

    kc_copy(1 - core).wait_recv()

    @pl.loop(0, 8)
    def _(e):
        kb_f[e, 0:HALF] = kb_all[0, e].astype(F32)
        kb_f[e, HALF : 2 * HALF] = kb_all[1, e].astype(F32)

    @pl.loop(0, 9)
    def _(ab):
        k0, k1, k2 = [
            kb_f[:, pl.ds(pl.multiple_of(ab * 24 + c * 8, 8), 8), :].reshape(64, 128) for c in range(3)
        ]
        this = jnp.concatenate([k1, k2], axis=0)
        last = jnp.concatenate([jnp.zeros((64, 128), F32), k0], axis=0)
        wb[ab] = jnp.concatenate([this, last], axis=1).astype(BF)
        vb[ab] = jnp.concatenate([this.T, last.T], axis=1).astype(BF)

    others(SLABS, mp, lambda i: ct_copy(i, i).wait_recv())
    order_row = lax.broadcasted_iota(jnp.int32, (512, 256), 0)
    order_col = lax.broadcasted_iota(jnp.int32, (512, 256), 1)
    order_pos = lax.rem(order_row, 256)
    order = (
        order_col == (lax.rem(order_pos, 16) + lax.div(order_row, 256)) * 16 + lax.div(order_pos, 16)
    ).astype(BF)
    for p in range(3):
        lanes = ct_all[:, :, p * 256 : p * 256 + 256].reshape(128, 256)
        both = dot_nt(order, lanes).astype(BF)
        cs[p, 0] = both[:256]
        cs[p, 1] = both[256:]
        cc[p] = jnp.concatenate([both[:256], earlier(both[:256])], axis=1)

    def slope(depth, rh, back):
        delta = back * jnp.where(pf[depth, rh] > 0, 1.0, 0.3)
        dd[depth, rh] = jnp.concatenate([delta, earlier(delta)], axis=1).astype(BF)

    for depth in range(2):
        for rd in range(2):
            for rh in range(2):
                along = [(1, 0)] if rd == 0 else [(2, 0), (0, 1)]
                down = [(1, 0)] if rh == 0 else [(2, 0), (0, 1)]
                lhs = [cs[depth + ahead, low] for _, ahead in along for _, low in down]
                rhs = [vb[a * 3 + b] for a, _ in along for b, _ in down]
                both = dot(jnp.concatenate(lhs, axis=1), jnp.concatenate(rhs, axis=0))
                back = (both[:, :128] + earlier(both[:, 128:])).astype(BF).astype(F32)
                if depth == 0 and rd == 0:
                    bk[rh] = back
                else:
                    slope(2 * depth + rd, rh, back)

    def grad_a_dot(a, depths):
        lhs = jnp.concatenate(
            [
                jnp.concatenate([xt[2 * depth + a, 2 * rh + b] for b in range(3)], axis=0)
                for depth in depths
                for rh in range(2)
            ],
            axis=1,
        )
        rhs = dd[depths[0] : depths[-1] + 1].reshape(512 * len(depths), 256)
        return dot(lhs, rhs)

    @pl.loop(0, 3)
    def _(a):
        acc_a[a] = grad_a_dot(a, (1, 2, 3))

    @pl.when(mp > 0)
    def _():
        x_halo().wait_recv()

    @pl.when(mp == 0)
    def _():
        xv[0] = jnp.zeros((64, 2048), BF)

    prepare(0)
    convolve(0)
    turn_x(0)
    for rh in range(2):
        slope(0, rh, bk[rh])

    lane = lax.broadcasted_iota(jnp.int32, (16, 128), 1)

    @pl.loop(0, 3)
    def _(a):
        acc = acc_a[a] + grad_a_dot(a, (0,))
        for b in range(3):
            this = acc[b * 128 : b * 128 + 128, :128]
            last = acc[b * 128 + 96 : b * 128 + 128, 128:]
            turned = pltpu.roll(this, 64, 1)
            sums = (last + turned[32:64], this[0:32] + turned[64:96], this[32:64] + turned[96:128])
            for c in range(3):
                packed = jnp.where(lane < 64, sums[c][:16], pltpu.roll(sums[c][16:], 64, 1))
                ga_f[pl.ds(pl.multiple_of(a * 144 + b * 48 + c * 16, 16), 16), :] = packed

    ga_f[432:512, :] = jnp.zeros((80, 128), F32)
    ga_s[...] = ga_f[...].reshape(GROUP, ROWS_A, 128).astype(BF)
    others(GROUP, me, lambda i: a1_copy(i, me).start())
    ga_1[me] = ga_s[me]

    def grad_b_rows(a, planes, cots):
        lhs = jnp.concatenate(
            [jnp.concatenate([ht[plane, b] for b in range(3)], axis=0) for plane in planes], axis=1
        )
        rhs = jnp.concatenate([cc[p] for p in cots], axis=0)
        acc = dot(lhs, rhs)
        for b in range(3):
            block = acc[b * 128 : b * 128 + 128]
            pieces = (block[64:, 128:], block[:64, :128], block[64:, :128])
            for c in range(3):
                start = a * 72 + b * 24 + c * 8
                gb_f[:, start : start + 8, :] = pieces[c].reshape(8, 8, 128)

    @pl.loop(0, 4)
    def _(index):
        turn_h(index)

    grad_b_rows(0, (1, 3), (1, 2))
    grad_b_rows(1, (0, 2), (0, 1))
    grad_b_rows(2, (1, 3), (0, 1))
    gb_f[:, 216:224, :] = jnp.zeros((8, 8, 128), F32)
    gb_s[...] = gb_f[:, pl.ds(pl.multiple_of((1 - core) * HALF, 8), HALF), :].astype(BF)
    b0_copy().start()

    def features_of(plane, terms):
        lhs = [hs[p, b] for p, _ in terms for b in range(3)]
        rhs = [wb[a * 3 + b] for _, a in terms for b in range(3)]
        both = dot(jnp.concatenate(lhs, axis=1), jnp.concatenate(rhs, axis=0))
        out = (both[:, :128] + later(both[:, 128:])).astype(BF)
        turned = dot_tn(out, order[:256]).astype(BF)
        ft[:, :, plane * 256 : plane * 256 + 256] = turned.reshape(8, 16, 256)

    features_of(0, [(0, 1), (1, 2)])
    b0_copy().wait_recv()
    own = pl.ds(pl.multiple_of(core * HALF, 8), HALF)
    gb_h[...] = (gb_f[:, own, :] + gb_0[...].astype(F32)).astype(BF)
    others(SLABS, mp, lambda i: b1_copy(i, mp).start())
    gb_1[mp] = gb_h[mp]
    features_of(1, [(1, 0), (2, 1), (3, 2)])
    features_of(2, [(3, 0)])
    others(SLABS, mp, lambda i: ft_copy(i, mp).start())
    fr[mp] = ft[mp]

    others(GROUP, me, lambda i: a1_copy(i, i).wait_recv())
    ga_2s[...] = jnp.sum(ga_1[...].astype(F32), axis=0)
    others(ring, rank, lambda i: a2_copy(i, rank).start())
    ga_2[rank] = ga_2s[...]

    others(SLABS, mp, lambda i: b1_copy(i, i).wait_recv())
    gb_2s[...] = jnp.sum(gb_1[...].astype(F32), axis=0).astype(BF)
    others(ring, rank, lambda i: b2_copy(i, rank).start())
    gb_2[rank] = gb_2s[...]

    others(ring, rank, lambda i: a2_copy(i, i).wait_recv())
    ga_3s[...] = (jnp.sum(ga_2[...], axis=0) * scale_a).astype(BF)
    others(GROUP, me, lambda i: a3_copy(i, me).start())
    ga_3[me] = ga_3s[...]

    others(SLABS, mp, lambda i: ft_copy(i, i).wait_recv())
    for e in range(SLABS):
        first = fr[e, :, 0:256].astype(F32)
        if e > 0:
            first = first + fr[e - 1, :, 512:768].astype(F32)
        planes = jnp.concatenate([first.astype(BF), fr[e, :, 256:512]], axis=1)
        feat[e * 512 : e * 512 + 512, :] = dot_tn(planes, eye).astype(BF)

    others(ring, rank, lambda i: b2_copy(i, i).wait_recv())
    gb_3[core] = jnp.sum(gb_2[...].astype(F32), axis=0) * scale_b
    b3_copy(core).start()

    @pl.when(mp < SLABS - 1)
    def _():
        x_halo().wait_send()

    others(SLABS, mp, lambda i: kb_copy(i, mp).wait_send())
    kc_copy(core).wait_send()
    others(SLABS, mp, lambda i: ct_copy(i, mp).wait_send())
    others(SLABS, mp, lambda i: ft_copy(i, mp).wait_send())
    b0_copy().wait_send()
    others(SLABS, mp, lambda i: b1_copy(i, mp).wait_send())
    others(ring, rank, lambda i: b2_copy(i, rank).wait_send())
    others(GROUP, me, lambda i: a1_copy(i, me).wait_send())
    others(ring, rank, lambda i: a2_copy(i, rank).wait_send())

    b3_copy(1 - core).wait_recv()
    gb[...] = gb_3[...]
    b3_copy(core).wait_send()
    others(GROUP, me, lambda i: a3_copy(i, i).wait_recv())
    ga[...] = ga_3[...]
    others(GROUP, me, lambda i: a3_copy(i, me).wait_send())


def finish(feat_in, ga_in, gb_in, feat, ga, gb, ga_v, sem):
    rest = 216 - HALF
    moves = [
        (feat_in, feat),
        (gb_in.at[0], gb.at[pl.ds(0, HALF)]),
        (gb_in.at[1, pl.ds(0, rest)], gb.at[pl.ds(HALF, rest)]),
        (ga_v, ga),
    ]
    copies = [pltpu.make_async_copy(src, dst, sem.at[place]) for place, (src, dst) in enumerate(moves)]
    for copy in copies[:-1]:
        copy.start()
    whole = ga_in[...].astype(F32).reshape(GROUP * ROWS_A, 128)[:432].reshape(27, 16, 128)
    ga_v[:, 0:16, :] = whole[:, :, :64]
    ga_v[:, 16:32, :] = whole[:, :, 64:]
    copies[-1].start()
    for copy in copies:
        copy.wait()


def hbm(array):
    return pltpu.with_memory_space_constraint(array, pltpu.HBM)


def shards(ring, samples, volume, kernel_a, kernel_b, cotangent):
    scale_a = 1.0 / math.sqrt(samples * 32**3)
    scale_b = 1.0 / math.sqrt(samples * 16**3)
    vmem = pltpu.VMEM
    dma = pltpu.SemaphoreType.DMA
    scratch = [
        vmem((9, 64, 2048), BF),
        vmem((9, 96, 64), BF),
        vmem((216, 128), BF),
        vmem((4096, 16), BF),
        vmem((9, 5, 256, 128), BF),
        vmem((9, 5, 128, 256), BF),
        vmem((9, 128, 256), BF),
        vmem((4, 2, 256, 128), F32),
        vmem((4, 3, 256, 128), BF),
        vmem((4, 3, 128, 256), BF),
        vmem((16, 4352), BF),
        vmem((8, 16, 768), BF),
        vmem((CORES, HALF, 128), BF),
        vmem((CORES, 8, HALF, 128), BF),
        vmem((8, 224, 128), F32),
        vmem((9, 128, 256), BF),
        vmem((9, 128, 256), BF),
        vmem((3, 2, 256, 128), BF),
        vmem((3, 256, 256), BF),
        vmem((8, 16, 768), BF),
        vmem((8, 16, 768), BF),
        vmem((4, 2, 256, 256), BF),
        vmem((2, 256, 128), F32),
        vmem((3, 384, 256), F32),
        vmem((8, 224, 128), F32),
        vmem((8, HALF, 128), BF),
        vmem((8, HALF, 128), BF),
        vmem((8, HALF, 128), BF),
        vmem((8, HALF, 128), BF),
        vmem((HALF, 128), BF),
        vmem((ring, HALF, 128), BF),
        vmem((CORES, HALF, 128), F32),
        vmem((512, 128), F32),
        vmem((GROUP, ROWS_A, 128), BF),
        vmem((GROUP, ROWS_A, 128), BF),
        vmem((ROWS_A, 128), F32),
        vmem((ring, ROWS_A, 128), F32),
        vmem((ROWS_A, 128), BF),
        vmem((GROUP, ROWS_A, 128), BF),
        dma((8,)),
        dma((3,)),
        dma,
        dma,
        dma((8,)),
        dma((8,)),
        dma((8,)),
        dma((8,)),
        dma,
        dma,
        dma((8,)),
        dma((8,)),
        dma,
        dma,
        dma((8,)),
        dma((8,)),
        dma((ring,)),
        dma((ring,)),
        dma,
        dma,
        dma((GROUP,)),
        dma((GROUP,)),
        dma((ring,)),
        dma((ring,)),
        dma((GROUP,)),
        dma((GROUP,)),
    ]
    in_vmem = pl.BlockSpec(memory_space=pltpu.VMEM)
    in_hbm = pl.BlockSpec(memory_space=pltpu.HBM)
    parts = pl.pallas_call(
        functools.partial(body, ring, scale_a, scale_b),
        out_shape=(
            jax.ShapeDtypeStruct((4096, 16), BF),
            jax.ShapeDtypeStruct((GROUP, ROWS_A, 128), BF),
            jax.ShapeDtypeStruct((CORES, HALF, 128), F32),
        ),
        in_specs=[in_hbm] * 4,
        out_specs=(in_vmem,) * 3,
        scratch_shapes=scratch,
        compiler_params=pltpu.CompilerParams(
            collective_id=0, has_side_effects=True, vmem_limit_bytes=48 * 1024 * 1024
        ),
        cost_estimate=pl.CostEstimate(flops=1600000000, bytes_accessed=4000000, transcendentals=0),
    )(
        hbm(volume.reshape(8, 64, 2048)),
        hbm(kernel_a.reshape(9, 96, 64)),
        hbm(kernel_b.reshape(216, 128)),
        hbm(cotangent.reshape(4096, 16)),
    )
    feat, ga, gb = pl.pallas_call(
        finish,
        out_shape=(
            jax.ShapeDtypeStruct((4096, 16), BF),
            jax.ShapeDtypeStruct((27, 32, 64), F32),
            jax.ShapeDtypeStruct((216, 128), F32),
        ),
        in_specs=[in_vmem] * 3,
        out_specs=(in_hbm, in_hbm, in_hbm),
        scratch_shapes=[vmem((27, 32, 64), F32), dma((4,))],
        compiler_params=pltpu.CompilerParams(vmem_limit_bytes=4 * 1024 * 1024),
    )(*parts)
    return (
        feat.reshape(1, 16, 16, 16, 16),
        ga.reshape(3, 3, 3, 32, 64),
        gb.reshape(3, 3, 3, 8, 128),
    )


def solution(mesh):
    ring = mesh.shape["dp"] // CORES
    return jax.shard_map(
        functools.partial(shards, ring, mesh.shape["dp"]),
        mesh=mesh,
        in_specs=(
            P("dp", "mp", None, None),
            P(),
            P(None, None, None, "mp", None),
            P("dp", None, None, None, "mp"),
        ),
        out_specs=(P("dp", None, None, None, "mp"), P(), P(None, None, None, "mp", None)),
        check_vma=False,
    )
```

```python
import functools
import math

import jax
import jax.numpy as jnp
from jax import lax
from jax.experimental import pallas as pl
from jax.experimental.pallas import tpu as pltpu
from jax.sharding import PartitionSpec as P

BF = jnp.bfloat16
F32 = jnp.float32
MESH = pl.DeviceIdType.MESH
SLABS = 8
CORES = 2
GROUP = SLABS * CORES
HALF = 112
ROWS_A = 32


def dot(lhs, rhs):
    return jnp.dot(lhs, rhs, preferred_element_type=F32)


def dot_nt(lhs, rhs):
    return lax.dot_general(lhs, rhs, (((1,), (1,)), ((), ())), preferred_element_type=F32)


def dot_tn(lhs, rhs):
    return lax.dot_general(lhs, rhs, (((0,), (0,)), ((), ())), preferred_element_type=F32)


def later(tiles):
    zero = jnp.zeros((16, tiles.shape[1]), tiles.dtype)
    return jnp.concatenate([zero, tiles[:-16]], axis=0)


def earlier(tiles):
    zero = jnp.zeros((16, tiles.shape[1]), tiles.dtype)
    return jnp.concatenate([tiles[16:], zero], axis=0)


def row_below(tiles):
    rolled = pltpu.roll(tiles.astype(F32), 1, 0)
    row = lax.broadcasted_iota(jnp.int32, tiles.shape, 0)
    return jnp.where(lax.rem(row, 16) == 0, 0.0, rolled).astype(BF)


def body(
    ring,
    scale_a,
    scale_b,
    x,
    ka_hbm,
    kb_hbm,
    cot_hbm,
    feat,
    ga,
    gb,
    xv,
    ka,
    kb,
    cot,
    xs,
    xt,
    wa,
    pf,
    hs,
    ht,
    ct_loc,
    ct_all,
    kb_half,
    kb_all,
    kb_f,
    wb,
    vb,
    cs,
    cc,
    ft,
    fr,
    dd,
    bk,
    acc_a,
    acc_x,
    gb_f,
    gb_s,
    gb_0,
    gb_h,
    gb_1,
    gb_2s,
    gb_2,
    gb_3,
    ga_f,
    ga_s,
    ga_1,
    ga_2s,
    ga_2,
    ga_3s,
    ga_3,
    x_sem,
    in_sem,
    xh_send,
    xh_recv,
    ct_send,
    ct_recv,
    kb_send,
    kb_recv,
    kc_send,
    kc_recv,
    ft_send,
    ft_recv,
    b0_send,
    b0_recv,
    b1_send,
    b1_recv,
    b2_send,
    b2_recv,
    b3_send,
    b3_recv,
    a1_send,
    a1_recv,
    a2_send,
    a2_recv,
    a3_send,
    a3_recv,
):
    mp = lax.axis_index("mp")
    dp = lax.axis_index("dp")
    core = lax.rem(dp, CORES)
    rank = lax.div(dp, CORES)
    me = mp * CORES + core

    def in_group(index):
        return {"mp": lax.div(index, CORES), "dp": rank * CORES + lax.rem(index, CORES)}

    def in_slabs(index):
        return {"mp": index, "dp": dp}

    def in_ring(index):
        return {"mp": mp, "dp": index * CORES + core}

    def others(size, mine, act):
        @pl.loop(1, size)
        def _(step):
            act(lax.rem(mine + step, size))

    def remote(src, dst, send, recv, device):
        return pltpu.make_async_remote_copy(
            src_ref=src, dst_ref=dst, send_sem=send, recv_sem=recv, device_id=device, device_id_type=MESH
        )

    def plane_copy(plane):
        return pltpu.make_async_copy(x.at[plane], xv.at[plane + 1], x_sem.at[plane])

    in_cot = pltpu.make_async_copy(cot_hbm, cot, in_sem.at[0])
    in_kb = pltpu.make_async_copy(kb_hbm, kb, in_sem.at[1])
    in_ka = pltpu.make_async_copy(ka_hbm, ka, in_sem.at[2])
    in_cot.start()
    in_kb.start()
    in_ka.start()

    @pl.loop(0, 8)
    def _(step):
        plane_copy(7 - step).start()

    barrier = pltpu.get_barrier_semaphore()
    others(GROUP, me, lambda i: pl.semaphore_signal(barrier, inc=1, device_id=in_group(i), device_id_type=MESH))
    others(ring, rank, lambda i: pl.semaphore_signal(barrier, inc=1, device_id=in_ring(i), device_id_type=MESH))

    in_kb.wait()
    in_ka.wait()
    in_cot.wait()

    eye = (
        lax.broadcasted_iota(jnp.int32, (16, 16), 0) == lax.broadcasted_iota(jnp.int32, (16, 16), 1)
    ).astype(BF)

    @pl.loop(0, 8)
    def _(pair):
        rows = cot[pl.ds(pl.multiple_of(pair * 512, 512), 512), :]
        ct_loc[:, pl.ds(pl.multiple_of(pair * 512, 512), 512)] = dot_nt(eye, rows).astype(BF)

    ct_loc[:, 4096:4352] = jnp.zeros((16, 256), BF)
    share = jnp.concatenate([kb[...].astype(F32), jnp.zeros((8, 128), F32)], axis=0).astype(BF)
    kb_half[0] = share[:HALF]
    kb_half[1] = share[HALF:]
    kb_all[core, mp] = kb_half[core]

    @pl.loop(0, 9)
    def _(ab):
        k0 = ka[ab, 0:32, :]
        k1 = ka[ab, 32:64, :]
        k2 = ka[ab, 64:96, :]
        no = jnp.zeros((32, 64), BF)
        wa[ab, 0:32, :] = jnp.concatenate([k1, no, no, no], axis=1)
        wa[ab, 32:64, :] = jnp.concatenate([k2, k0, no, no], axis=1)
        wa[ab, 64:96, :] = jnp.concatenate([no, k1, no, no], axis=1)
        wa[ab, 96:128, :] = jnp.concatenate([no, k2, k0, no], axis=1)

    pick_row = lax.broadcasted_iota(jnp.int32, (80, 64), 0)
    pick_col = lax.broadcasted_iota(jnp.int32, (80, 64), 1)
    pick = (pick_col == 4 * lax.rem(pick_row, 16) + lax.div(pick_row, 16) - 1).astype(BF)

    def prepare(index):
        rows = dot(pick, xv[index]).astype(BF)
        for s in range(5):
            for q in range(16):
                xs[index, s, q * 16 : q * 16 + 16, :] = rows[s * 16 : s * 16 + 16, q * 128 : q * 128 + 128]

    def conv_dot(depth, rh, offsets):
        parts = [xs[2 * depth + a, 2 * rh + b] for a in offsets for b in range(3)]
        weights = wa[3 * offsets[0] : 3 * offsets[-1] + 3].reshape(3 * len(offsets) * 128, 256)
        return dot(jnp.concatenate(parts, axis=1), weights)

    def convolve(depth, begun=None):
        for rh in range(2):
            if begun is None:
                both = conv_dot(depth, rh, (0, 1, 2))
            else:
                both = conv_dot(depth, rh, (0,)) + begun[rh]
            pre = both[:, :128] + later(both[:, 128:])
            pf[depth, rh] = pre
            hidden = jnp.where(pre > 0, pre, 0.3 * pre).astype(BF)
            hs[depth, rh + 1] = hidden
            if rh == 1:
                hs[depth, 0] = row_below(hidden)

    def both_planes(depth):
        plane_copy(2 * depth).wait()
        prepare(2 * depth + 1)
        plane_copy(2 * depth - 1).wait()
        prepare(2 * depth)
        convolve(depth)

    pl.semaphore_wait(barrier, GROUP - 1 + ring - 1)

    def x_halo():
        return remote(x.at[7], xv.at[0], xh_send, xh_recv, in_slabs(mp + 1))

    def ct_copy(peer, slot):
        src = ct_loc.at[:, pl.ds(pl.multiple_of(peer * 512, 512), 768)]
        return remote(src, ct_all.at[slot], ct_send.at[peer], ct_recv.at[slot], in_slabs(peer))

    def kb_copy(peer, slot):
        return remote(
            kb_all.at[core, mp], kb_all.at[core, slot], kb_send.at[peer], kb_recv.at[slot], in_slabs(peer)
        )

    def kc_copy(half):
        return remote(kb_all.at[half], kb_all.at[half], kc_send, kc_recv, in_group(mp * CORES + 1 - core))

    def ft_copy(peer, slot):
        return remote(ft.at[peer], fr.at[slot], ft_send.at[peer], ft_recv.at[slot], in_slabs(peer))

    def b0_copy():
        return remote(gb_s, gb_0, b0_send, b0_recv, in_group(mp * CORES + 1 - core))

    def b1_copy(peer, slot):
        return remote(gb_h.at[peer], gb_1.at[slot], b1_send.at[peer], b1_recv.at[slot], in_slabs(peer))

    def b2_copy(peer, slot):
        return remote(gb_2s, gb_2.at[slot], b2_send.at[peer], b2_recv.at[slot], in_ring(peer))

    def b3_copy(slot):
        return remote(gb_3.at[core], gb_3.at[slot], b3_send, b3_recv, in_group(mp * CORES + 1 - core))

    def a1_copy(peer, slot):
        return remote(ga_s.at[peer], ga_1.at[slot], a1_send.at[peer], a1_recv.at[slot], in_group(peer))

    def a2_copy(peer, slot):
        return remote(ga_2s, ga_2.at[slot], a2_send.at[peer], a2_recv.at[slot], in_ring(peer))

    def a3_copy(peer, slot):
        return remote(ga_3s, ga_3.at[slot], a3_send.at[peer], a3_recv.at[slot], in_group(peer))

    others(SLABS, mp, lambda i: kb_copy(i, mp).start())
    others(SLABS, mp, lambda i: ct_copy(i, mp).start())

    @pl.when(mp < SLABS - 1)
    def _():
        x_halo().start()

    ct_all[mp] = ct_loc[:, pl.ds(pl.multiple_of(mp * 512, 512), 768)]

    plane_copy(7).wait()
    prepare(8)
    both_planes(3)

    @pl.loop(0, 2)
    def _(step):
        both_planes(2 - step)

    plane_copy(0).wait()
    prepare(1)
    for rh in range(2):
        acc_x[rh] = conv_dot(0, rh, (1, 2))

    def turn_x(index):
        for s in range(5):
            xt[index, s] = xs[index, s].T

    def turn_h(index):
        for b in range(3):
            ht[index, b] = hs[index, b].T

    @pl.loop(1, 9)
    def _(index):
        turn_x(index)

    others(SLABS, mp, lambda i: kb_copy(i, i).wait_recv())
    kc_copy(core).start()

    kc_copy(1 - core).wait_recv()

    @pl.loop(0, 8)
    def _(e):
        kb_f[e, 0:HALF] = kb_all[0, e].astype(F32)
        kb_f[e, HALF : 2 * HALF] = kb_all[1, e].astype(F32)

    @pl.loop(0, 9)
    def _(ab):
        k0, k1, k2 = [
            kb_f[:, pl.ds(pl.multiple_of(ab * 24 + c * 8, 8), 8), :].reshape(64, 128) for c in range(3)
        ]
        this = jnp.concatenate([k1, k2], axis=0)
        last = jnp.concatenate([jnp.zeros((64, 128), F32), k0], axis=0)
        wb[ab] = jnp.concatenate([this, last], axis=1).astype(BF)
        vb[ab] = jnp.concatenate([this.T, last.T], axis=1).astype(BF)

    others(SLABS, mp, lambda i: ct_copy(i, i).wait_recv())
    order_row = lax.broadcasted_iota(jnp.int32, (512, 256), 0)
    order_col = lax.broadcasted_iota(jnp.int32, (512, 256), 1)
    order_pos = lax.rem(order_row, 256)
    order = (
        order_col == (lax.rem(order_pos, 16) + lax.div(order_row, 256)) * 16 + lax.div(order_pos, 16)
    ).astype(BF)
    for p in range(3):
        lanes = ct_all[:, :, p * 256 : p * 256 + 256].reshape(128, 256)
        both = dot_nt(order, lanes).astype(BF)
        cs[p, 0] = both[:256]
        cs[p, 1] = both[256:]
        cc[p] = jnp.concatenate([both[:256], earlier(both[:256])], axis=1)

    def slope(depth, rh, back):
        delta = back * jnp.where(pf[depth, rh] > 0, 1.0, 0.3)
        dd[depth, rh] = jnp.concatenate([delta, earlier(delta)], axis=1).astype(BF)

    for depth in range(2):
        for rd in range(2):
            for rh in range(2):
                along = [(1, 0)] if rd == 0 else [(2, 0), (0, 1)]
                down = [(1, 0)] if rh == 0 else [(2, 0), (0, 1)]
                lhs = [cs[depth + ahead, low] for _, ahead in along for _, low in down]
                rhs = [vb[a * 3 + b] for a, _ in along for b, _ in down]
                both = dot(jnp.concatenate(lhs, axis=1), jnp.concatenate(rhs, axis=0))
                back = (both[:, :128] + earlier(both[:, 128:])).astype(BF).astype(F32)
                if depth == 0 and rd == 0:
                    bk[rh] = back
                else:
                    slope(2 * depth + rd, rh, back)

    def grad_a_dot(a, depths):
        lhs = jnp.concatenate(
            [
                jnp.concatenate([xt[2 * depth + a, 2 * rh + b] for b in range(3)], axis=0)
                for depth in depths
                for rh in range(2)
            ],
            axis=1,
        )
        rhs = dd[depths[0] : depths[-1] + 1].reshape(512 * len(depths), 256)
        return dot(lhs, rhs)

    @pl.loop(0, 3)
    def _(a):
        acc_a[a] = grad_a_dot(a, (1, 2, 3))

    @pl.when(mp > 0)
    def _():
        x_halo().wait_recv()

    @pl.when(mp == 0)
    def _():
        xv[0] = jnp.zeros((64, 2048), BF)

    prepare(0)
    convolve(0, acc_x)
    turn_x(0)
    for rh in range(2):
        slope(0, rh, bk[rh])

    lane = lax.broadcasted_iota(jnp.int32, (16, 128), 1)

    @pl.loop(0, 3)
    def _(a):
        acc = acc_a[a] + grad_a_dot(a, (0,))
        for b in range(3):
            this = acc[b * 128 : b * 128 + 128, :128]
            last = acc[b * 128 + 96 : b * 128 + 128, 128:]
            turned = pltpu.roll(this, 64, 1)
            sums = (last + turned[32:64], this[0:32] + turned[64:96], this[32:64] + turned[96:128])
            for c in range(3):
                packed = jnp.where(lane < 64, sums[c][:16], pltpu.roll(sums[c][16:], 64, 1))
                ga_f[pl.ds(pl.multiple_of(a * 144 + b * 48 + c * 16, 16), 16), :] = packed

    ga_f[432:512, :] = jnp.zeros((80, 128), F32)
    ga_s[...] = ga_f[...].reshape(GROUP, ROWS_A, 128).astype(BF)
    others(GROUP, me, lambda i: a1_copy(i, me).start())
    ga_1[me] = ga_s[me]

    def grad_b_rows(a, planes, cots):
        lhs = jnp.concatenate(
            [jnp.concatenate([ht[plane, b] for b in range(3)], axis=0) for plane in planes], axis=1
        )
        rhs = jnp.concatenate([cc[p] for p in cots], axis=0)
        acc = dot(lhs, rhs)
        for b in range(3):
            block = acc[b * 128 : b * 128 + 128]
            pieces = (block[64:, 128:], block[:64, :128], block[64:, :128])
            for c in range(3):
                start = a * 72 + b * 24 + c * 8
                gb_f[:, start : start + 8, :] = pieces[c].reshape(8, 8, 128)

    @pl.loop(0, 4)
    def _(index):
        turn_h(index)

    grad_b_rows(0, (1, 3), (1, 2))
    grad_b_rows(1, (0, 2), (0, 1))
    grad_b_rows(2, (1, 3), (0, 1))
    gb_f[:, 216:224, :] = jnp.zeros((8, 8, 128), F32)
    gb_s[...] = gb_f[:, pl.ds(pl.multiple_of((1 - core) * HALF, 8), HALF), :].astype(BF)
    b0_copy().start()

    def features_of(plane, terms):
        lhs = [hs[p, b] for p, _ in terms for b in range(3)]
        rhs = [wb[a * 3 + b] for _, a in terms for b in range(3)]
        both = dot(jnp.concatenate(lhs, axis=1), jnp.concatenate(rhs, axis=0))
        out = (both[:, :128] + later(both[:, 128:])).astype(BF)
        turned = dot_tn(out, order[:256]).astype(BF)
        ft[:, :, plane * 256 : plane * 256 + 256] = turned.reshape(8, 16, 256)

    features_of(0, [(0, 1), (1, 2)])
    b0_copy().wait_recv()
    own = pl.ds(pl.multiple_of(core * HALF, 8), HALF)
    gb_h[...] = (gb_f[:, own, :] + gb_0[...].astype(F32)).astype(BF)
    others(SLABS, mp, lambda i: b1_copy(i, mp).start())
    gb_1[mp] = gb_h[mp]
    features_of(1, [(1, 0), (2, 1), (3, 2)])
    features_of(2, [(3, 0)])
    others(SLABS, mp, lambda i: ft_copy(i, mp).start())
    fr[mp] = ft[mp]

    others(GROUP, me, lambda i: a1_copy(i, i).wait_recv())
    ga_2s[...] = jnp.sum(ga_1[...].astype(F32), axis=0)
    others(ring, rank, lambda i: a2_copy(i, rank).start())
    ga_2[rank] = ga_2s[...]

    others(SLABS, mp, lambda i: b1_copy(i, i).wait_recv())
    gb_2s[...] = jnp.sum(gb_1[...].astype(F32), axis=0).astype(BF)
    others(ring, rank, lambda i: b2_copy(i, rank).start())
    gb_2[rank] = gb_2s[...]

    others(ring, rank, lambda i: a2_copy(i, i).wait_recv())
    ga_3s[...] = (jnp.sum(ga_2[...], axis=0) * scale_a).astype(BF)
    others(GROUP, me, lambda i: a3_copy(i, me).start())
    ga_3[me] = ga_3s[...]

    others(ring, rank, lambda i: b2_copy(i, i).wait_recv())
    gb_3[core] = jnp.sum(gb_2[...].astype(F32), axis=0) * scale_b
    b3_copy(core).start()

    others(SLABS, mp, lambda i: ft_copy(i, i).wait_recv())
    for e in range(SLABS):
        first = fr[e, :, 0:256].astype(F32)
        if e > 0:
            first = first + fr[e - 1, :, 512:768].astype(F32)
        planes = jnp.concatenate([first.astype(BF), fr[e, :, 256:512]], axis=1)
        feat[e * 512 : e * 512 + 512, :] = dot_tn(planes, eye).astype(BF)

    @pl.when(mp < SLABS - 1)
    def _():
        x_halo().wait_send()

    others(SLABS, mp, lambda i: kb_copy(i, mp).wait_send())
    kc_copy(core).wait_send()
    others(SLABS, mp, lambda i: ct_copy(i, mp).wait_send())
    others(SLABS, mp, lambda i: ft_copy(i, mp).wait_send())
    b0_copy().wait_send()
    others(SLABS, mp, lambda i: b1_copy(i, mp).wait_send())
    others(ring, rank, lambda i: b2_copy(i, rank).wait_send())
    others(GROUP, me, lambda i: a1_copy(i, me).wait_send())
    others(ring, rank, lambda i: a2_copy(i, rank).wait_send())

    b3_copy(1 - core).wait_recv()
    gb[...] = gb_3[...]
    b3_copy(core).wait_send()
    others(GROUP, me, lambda i: a3_copy(i, me).wait_send())
    others(GROUP, me, lambda i: a3_copy(i, i).wait_recv())
    ga[...] = ga_3[...]


def finish(feat_in, ga_in, gb_in, feat, ga, gb, ga_v, sem):
    rest = 216 - HALF
    moves = [
        (feat_in, feat),
        (gb_in.at[0], gb.at[pl.ds(0, HALF)]),
        (gb_in.at[1, pl.ds(0, rest)], gb.at[pl.ds(HALF, rest)]),
        (ga_v, ga),
    ]
    copies = [pltpu.make_async_copy(src, dst, sem.at[place]) for place, (src, dst) in enumerate(moves)]
    for copy in copies[:-1]:
        copy.start()
    whole = ga_in[...].astype(F32).reshape(GROUP * ROWS_A, 128)[:432].reshape(27, 16, 128)
    ga_v[:, 0:16, :] = whole[:, :, :64]
    ga_v[:, 16:32, :] = whole[:, :, 64:]
    copies[-1].start()
    for copy in copies:
        copy.wait()


def hbm(array):
    return pltpu.with_memory_space_constraint(array, pltpu.HBM)


def shards(ring, samples, volume, kernel_a, kernel_b, cotangent):
    scale_a = 1.0 / math.sqrt(samples * 32**3)
    scale_b = 1.0 / math.sqrt(samples * 16**3)
    vmem = pltpu.VMEM
    dma = pltpu.SemaphoreType.DMA
    scratch = [
        vmem((9, 64, 2048), BF),
        vmem((9, 96, 64), BF),
        vmem((216, 128), BF),
        vmem((4096, 16), BF),
        vmem((9, 5, 256, 128), BF),
        vmem((9, 5, 128, 256), BF),
        vmem((9, 128, 256), BF),
        vmem((4, 2, 256, 128), F32),
        vmem((4, 3, 256, 128), BF),
        vmem((4, 3, 128, 256), BF),
        vmem((16, 4352), BF),
        vmem((8, 16, 768), BF),
        vmem((CORES, HALF, 128), BF),
        vmem((CORES, 8, HALF, 128), BF),
        vmem((8, 224, 128), F32),
        vmem((9, 128, 256), BF),
        vmem((9, 128, 256), BF),
        vmem((3, 2, 256, 128), BF),
        vmem((3, 256, 256), BF),
        vmem((8, 16, 768), BF),
        vmem((8, 16, 768), BF),
        vmem((4, 2, 256, 256), BF),
        vmem((2, 256, 128), F32),
        vmem((3, 384, 256), F32),
        vmem((2, 256, 256), F32),
        vmem((8, 224, 128), F32),
        vmem((8, HALF, 128), BF),
        vmem((8, HALF, 128), BF),
        vmem((8, HALF, 128), BF),
        vmem((8, HALF, 128), BF),
        vmem((HALF, 128), BF),
        vmem((ring, HALF, 128), BF),
        vmem((CORES, HALF, 128), F32),
        vmem((512, 128), F32),
        vmem((GROUP, ROWS_A, 128), BF),
        vmem((GROUP, ROWS_A, 128), BF),
        vmem((ROWS_A, 128), F32),
        vmem((ring, ROWS_A, 128), F32),
        vmem((ROWS_A, 128), BF),
        vmem((GROUP, ROWS_A, 128), BF),
        dma((8,)),
        dma((3,)),
        dma,
        dma,
        dma((8,)),
        dma((8,)),
        dma((8,)),
        dma((8,)),
        dma,
        dma,
        dma((8,)),
        dma((8,)),
        dma,
        dma,
        dma((8,)),
        dma((8,)),
        dma((ring,)),
        dma((ring,)),
        dma,
        dma,
        dma((GROUP,)),
        dma((GROUP,)),
        dma((ring,)),
        dma((ring,)),
        dma((GROUP,)),
        dma((GROUP,)),
    ]
    in_vmem = pl.BlockSpec(memory_space=pltpu.VMEM)
    in_hbm = pl.BlockSpec(memory_space=pltpu.HBM)
    parts = pl.pallas_call(
        functools.partial(body, ring, scale_a, scale_b),
        out_shape=(
            jax.ShapeDtypeStruct((4096, 16), BF),
            jax.ShapeDtypeStruct((GROUP, ROWS_A, 128), BF),
            jax.ShapeDtypeStruct((CORES, HALF, 128), F32),
        ),
        in_specs=[in_hbm] * 4,
        out_specs=(in_vmem,) * 3,
        scratch_shapes=scratch,
        compiler_params=pltpu.CompilerParams(
            collective_id=0, has_side_effects=True, vmem_limit_bytes=48 * 1024 * 1024
        ),
        cost_estimate=pl.CostEstimate(flops=1600000000, bytes_accessed=4000000, transcendentals=0),
    )(
        hbm(volume.reshape(8, 64, 2048)),
        hbm(kernel_a.reshape(9, 96, 64)),
        hbm(kernel_b.reshape(216, 128)),
        hbm(cotangent.reshape(4096, 16)),
    )
    feat, ga, gb = pl.pallas_call(
        finish,
        out_shape=(
            jax.ShapeDtypeStruct((4096, 16), BF),
            jax.ShapeDtypeStruct((27, 32, 64), F32),
            jax.ShapeDtypeStruct((216, 128), F32),
        ),
        in_specs=[in_vmem] * 3,
        out_specs=(in_hbm, in_hbm, in_hbm),
        scratch_shapes=[vmem((27, 32, 64), F32), dma((4,))],
        compiler_params=pltpu.CompilerParams(vmem_limit_bytes=4 * 1024 * 1024),
    )(*parts)
    return (
        feat.reshape(1, 16, 16, 16, 16),
        ga.reshape(3, 3, 3, 32, 64),
        gb.reshape(3, 3, 3, 8, 128),
    )


def solution(mesh):
    ring = mesh.shape["dp"] // CORES
    return jax.shard_map(
        functools.partial(shards, ring, mesh.shape["dp"]),
        mesh=mesh,
        in_specs=(
            P("dp", "mp", None, None),
            P(),
            P(None, None, None, "mp", None),
            P("dp", None, None, None, "mp"),
        ),
        out_specs=(P("dp", None, None, None, "mp"), P(), P(None, None, None, "mp", None)),
        check_vma=False,
    )
```

```python
import functools
import math

import jax
import jax.numpy as jnp
from jax import lax
from jax.experimental import pallas as pl
from jax.experimental.pallas import tpu as pltpu
from jax.sharding import PartitionSpec as P

BF = jnp.bfloat16
F32 = jnp.float32
MESH = pl.DeviceIdType.MESH
SLABS = 8
CORES = 2
GROUP = SLABS * CORES
HALF = 112
ROWS_A = 32


def dot(lhs, rhs):
    return jnp.dot(lhs, rhs, preferred_element_type=F32)


def dot_nt(lhs, rhs):
    return lax.dot_general(lhs, rhs, (((1,), (1,)), ((), ())), preferred_element_type=F32)


def dot_tn(lhs, rhs):
    return lax.dot_general(lhs, rhs, (((0,), (0,)), ((), ())), preferred_element_type=F32)


def later(tiles):
    zero = jnp.zeros((16, tiles.shape[1]), tiles.dtype)
    return jnp.concatenate([zero, tiles[:-16]], axis=0)


def earlier(tiles):
    zero = jnp.zeros((16, tiles.shape[1]), tiles.dtype)
    return jnp.concatenate([tiles[16:], zero], axis=0)


def row_below(tiles):
    rolled = pltpu.roll(tiles.astype(F32), 1, 0)
    row = lax.broadcasted_iota(jnp.int32, tiles.shape, 0)
    return jnp.where(lax.rem(row, 16) == 0, 0.0, rolled).astype(BF)


def body(
    ring,
    scale_a,
    scale_b,
    x,
    ka_hbm,
    kb_hbm,
    cot_hbm,
    feat,
    ga,
    gb,
    xv,
    ka,
    kb,
    cot,
    xs,
    xt,
    wa,
    pf,
    hs,
    ht,
    ct_loc,
    ct_all,
    kb_half,
    kb_all,
    kb_f,
    wb,
    vb,
    cs,
    cc,
    ft,
    fr,
    dd,
    bk,
    acc_a,
    acc_x,
    gb_f,
    gb_s,
    gb_0,
    gb_h,
    gb_1,
    gb_2s,
    gb_2,
    gb_3,
    ga_f,
    ga_s,
    ga_1,
    ga_2s,
    ga_2,
    ga_3s,
    ga_3,
    x_sem,
    in_sem,
    xh_send,
    xh_recv,
    ct_send,
    ct_recv,
    kb_send,
    kb_recv,
    kc_send,
    kc_recv,
    ft_send,
    ft_recv,
    b0_send,
    b0_recv,
    b1_send,
    b1_recv,
    b2_send,
    b2_recv,
    b3_send,
    b3_recv,
    a1_send,
    a1_recv,
    a2_send,
    a2_recv,
    a3_send,
    a3_recv,
):
    mp = lax.axis_index("mp")
    dp = lax.axis_index("dp")
    core = lax.rem(dp, CORES)
    rank = lax.div(dp, CORES)
    me = mp * CORES + core

    def in_group(index):
        return {"mp": lax.div(index, CORES), "dp": rank * CORES + lax.rem(index, CORES)}

    def in_slabs(index):
        return {"mp": index, "dp": dp}

    def in_ring(index):
        return {"mp": mp, "dp": index * CORES + core}

    def others(size, mine, act):
        @pl.loop(1, size)
        def _(step):
            act(lax.rem(mine + step, size))

    def remote(src, dst, send, recv, device):
        return pltpu.make_async_remote_copy(
            src_ref=src, dst_ref=dst, send_sem=send, recv_sem=recv, device_id=device, device_id_type=MESH
        )

    def plane_copy(plane):
        return pltpu.make_async_copy(x.at[plane], xv.at[plane + 1], x_sem.at[plane])

    in_cot = pltpu.make_async_copy(cot_hbm, cot, in_sem.at[0])
    in_kb = pltpu.make_async_copy(kb_hbm, kb, in_sem.at[1])
    in_ka = pltpu.make_async_copy(ka_hbm, ka, in_sem.at[2])
    in_cot.start()
    in_kb.start()
    in_ka.start()

    @pl.loop(0, 8)
    def _(step):
        plane_copy(7 - step).start()

    barrier = pltpu.get_barrier_semaphore()
    others(GROUP, me, lambda i: pl.semaphore_signal(barrier, inc=1, device_id=in_group(i), device_id_type=MESH))
    others(ring, rank, lambda i: pl.semaphore_signal(barrier, inc=1, device_id=in_ring(i), device_id_type=MESH))

    in_kb.wait()
    in_ka.wait()
    in_cot.wait()

    eye = (
        lax.broadcasted_iota(jnp.int32, (16, 16), 0) == lax.broadcasted_iota(jnp.int32, (16, 16), 1)
    ).astype(BF)

    @pl.loop(0, 8)
    def _(pair):
        rows = cot[pl.ds(pl.multiple_of(pair * 512, 512), 512), :]
        ct_loc[:, pl.ds(pl.multiple_of(pair * 512, 512), 512)] = dot_nt(eye, rows).astype(BF)

    ct_loc[:, 4096:4352] = jnp.zeros((16, 256), BF)
    share = jnp.concatenate([kb[...].astype(F32), jnp.zeros((8, 128), F32)], axis=0).astype(BF)
    kb_half[0] = share[:HALF]
    kb_half[1] = share[HALF:]
    kb_all[core, mp] = kb_half[core]

    @pl.loop(0, 9)
    def _(ab):
        k0 = ka[ab, 0:32, :]
        k1 = ka[ab, 32:64, :]
        k2 = ka[ab, 64:96, :]
        no = jnp.zeros((32, 64), BF)
        wa[ab, 0:32, :] = jnp.concatenate([k1, no, no, no], axis=1)
        wa[ab, 32:64, :] = jnp.concatenate([k2, k0, no, no], axis=1)
        wa[ab, 64:96, :] = jnp.concatenate([no, k1, no, no], axis=1)
        wa[ab, 96:128, :] = jnp.concatenate([no, k2, k0, no], axis=1)

    pick_row = lax.broadcasted_iota(jnp.int32, (80, 64), 0)
    pick_col = lax.broadcasted_iota(jnp.int32, (80, 64), 1)
    pick = (pick_col == 4 * lax.rem(pick_row, 16) + lax.div(pick_row, 16) - 1).astype(BF)

    def prepare(index):
        rows = dot(pick, xv[index]).astype(BF)
        for s in range(5):
            for q in range(16):
                xs[index, s, q * 16 : q * 16 + 16, :] = rows[s * 16 : s * 16 + 16, q * 128 : q * 128 + 128]

    def conv_dot(depth, rh, offsets):
        parts = [xs[2 * depth + a, 2 * rh + b] for a in offsets for b in range(3)]
        weights = wa[3 * offsets[0] : 3 * offsets[-1] + 3].reshape(3 * len(offsets) * 128, 256)
        return dot(jnp.concatenate(parts, axis=1), weights)

    def convolve(depth, begun=None):
        for rh in range(2):
            if begun is None:
                both = conv_dot(depth, rh, (0, 1, 2))
            else:
                both = conv_dot(depth, rh, (0,)) + begun[rh]
            pre = both[:, :128] + later(both[:, 128:])
            pf[depth, rh] = pre
            hidden = jnp.where(pre > 0, pre, 0.3 * pre).astype(BF)
            hs[depth, rh + 1] = hidden
            if rh == 1:
                hs[depth, 0] = row_below(hidden)

    def both_planes(depth):
        plane_copy(2 * depth).wait()
        prepare(2 * depth + 1)
        plane_copy(2 * depth - 1).wait()
        prepare(2 * depth)
        convolve(depth)

    pl.semaphore_wait(barrier, GROUP - 1 + ring - 1)

    def x_halo():
        return remote(x.at[7], xv.at[0], xh_send, xh_recv, in_slabs(mp + 1))

    def ct_copy(peer, slot):
        src = ct_loc.at[:, pl.ds(pl.multiple_of(peer * 512, 512), 768)]
        return remote(src, ct_all.at[slot], ct_send.at[peer], ct_recv.at[slot], in_slabs(peer))

    def kb_copy(peer, slot):
        return remote(
            kb_all.at[core, mp], kb_all.at[core, slot], kb_send.at[peer], kb_recv.at[slot], in_slabs(peer)
        )

    def kc_copy(half):
        return remote(kb_all.at[half], kb_all.at[half], kc_send, kc_recv, in_group(mp * CORES + 1 - core))

    def ft_copy(peer, slot):
        return remote(ft.at[peer], fr.at[slot], ft_send.at[peer], ft_recv.at[slot], in_slabs(peer))

    def b0_copy():
        return remote(gb_s, gb_0, b0_send, b0_recv, in_group(mp * CORES + 1 - core))

    def b1_copy(peer, slot):
        return remote(gb_h.at[peer], gb_1.at[slot], b1_send.at[peer], b1_recv.at[slot], in_slabs(peer))

    def b2_copy(peer, slot):
        return remote(gb_2s, gb_2.at[slot], b2_send.at[peer], b2_recv.at[slot], in_ring(peer))

    def b3_copy(slot):
        return remote(gb_3.at[core], gb_3.at[slot], b3_send, b3_recv, in_group(mp * CORES + 1 - core))

    def a1_copy(peer, slot):
        return remote(ga_s.at[peer], ga_1.at[slot], a1_send.at[peer], a1_recv.at[slot], in_group(peer))

    def a2_copy(peer, slot):
        return remote(ga_2s, ga_2.at[slot], a2_send.at[peer], a2_recv.at[slot], in_ring(peer))

    def a3_copy(peer, slot):
        return remote(ga_3s, ga_3.at[slot], a3_send.at[peer], a3_recv.at[slot], in_group(peer))

    others(SLABS, mp, lambda i: kb_copy(i, mp).start())
    others(SLABS, mp, lambda i: ct_copy(i, mp).start())

    @pl.when(mp < SLABS - 1)
    def _():
        x_halo().start()

    ct_all[mp] = ct_loc[:, pl.ds(pl.multiple_of(mp * 512, 512), 768)]

    plane_copy(7).wait()
    prepare(8)
    both_planes(3)

    @pl.loop(0, 2)
    def _(step):
        both_planes(2 - step)

    plane_copy(0).wait()
    prepare(1)
    for rh in range(2):
        acc_x[rh] = conv_dot(0, rh, (1, 2))

    def turn_x(index):
        for s in range(5):
            xt[index, s] = xs[index, s].T

    def turn_h(index):
        for b in range(3):
            ht[index, b] = hs[index, b].T

    @pl.loop(1, 9)
    def _(index):
        turn_x(index)

    @pl.loop(1, 4)
    def _(index):
        turn_h(index)

    others(SLABS, mp, lambda i: kb_copy(i, i).wait_recv())
    kc_copy(core).start()

    kc_copy(1 - core).wait_recv()

    @pl.loop(0, 8)
    def _(e):
        kb_f[e, 0:HALF] = kb_all[0, e].astype(F32)
        kb_f[e, HALF : 2 * HALF] = kb_all[1, e].astype(F32)

    @pl.loop(0, 9)
    def _(ab):
        k0, k1, k2 = [
            kb_f[:, pl.ds(pl.multiple_of(ab * 24 + c * 8, 8), 8), :].reshape(64, 128) for c in range(3)
        ]
        this = jnp.concatenate([k1, k2], axis=0)
        last = jnp.concatenate([jnp.zeros((64, 128), F32), k0], axis=0)
        wb[ab] = jnp.concatenate([this, last], axis=1).astype(BF)
        vb[ab] = jnp.concatenate([this.T, last.T], axis=1).astype(BF)

    others(SLABS, mp, lambda i: ct_copy(i, i).wait_recv())
    order_row = lax.broadcasted_iota(jnp.int32, (512, 256), 0)
    order_col = lax.broadcasted_iota(jnp.int32, (512, 256), 1)
    order_pos = lax.rem(order_row, 256)
    order = (
        order_col == (lax.rem(order_pos, 16) + lax.div(order_row, 256)) * 16 + lax.div(order_pos, 16)
    ).astype(BF)
    for p in range(3):
        lanes = ct_all[:, :, p * 256 : p * 256 + 256].reshape(128, 256)
        both = dot_nt(order, lanes).astype(BF)
        cs[p, 0] = both[:256]
        cs[p, 1] = both[256:]
        cc[p] = jnp.concatenate([both[:256], earlier(both[:256])], axis=1)

    def slope(depth, rh, back):
        delta = back * jnp.where(pf[depth, rh] > 0, 1.0, 0.3)
        dd[depth, rh] = jnp.concatenate([delta, earlier(delta)], axis=1).astype(BF)

    for depth in range(2):
        for rd in range(2):
            for rh in range(2):
                along = [(1, 0)] if rd == 0 else [(2, 0), (0, 1)]
                down = [(1, 0)] if rh == 0 else [(2, 0), (0, 1)]
                lhs = [cs[depth + ahead, low] for _, ahead in along for _, low in down]
                rhs = [vb[a * 3 + b] for a, _ in along for b, _ in down]
                both = dot(jnp.concatenate(lhs, axis=1), jnp.concatenate(rhs, axis=0))
                back = (both[:, :128] + earlier(both[:, 128:])).astype(BF).astype(F32)
                if depth == 0 and rd == 0:
                    bk[rh] = back
                else:
                    slope(2 * depth + rd, rh, back)

    def grad_a_dot(a, depths):
        lhs = jnp.concatenate(
            [
                jnp.concatenate([xt[2 * depth + a, 2 * rh + b] for b in range(3)], axis=0)
                for depth in depths
                for rh in range(2)
            ],
            axis=1,
        )
        rhs = dd[depths[0] : depths[-1] + 1].reshape(512 * len(depths), 256)
        return dot(lhs, rhs)

    @pl.loop(0, 3)
    def _(a):
        acc_a[a] = grad_a_dot(a, (1, 2, 3))

    def grad_b_rows(a, planes, cots):
        lhs = jnp.concatenate(
            [jnp.concatenate([ht[plane, b] for b in range(3)], axis=0) for plane in planes], axis=1
        )
        rhs = jnp.concatenate([cc[p] for p in cots], axis=0)
        acc = dot(lhs, rhs)
        for b in range(3):
            block = acc[b * 128 : b * 128 + 128]
            pieces = (block[64:, 128:], block[:64, :128], block[64:, :128])
            for c in range(3):
                start = a * 72 + b * 24 + c * 8
                gb_f[:, start : start + 8, :] = pieces[c].reshape(8, 8, 128)

    grad_b_rows(0, (1, 3), (1, 2))
    grad_b_rows(2, (1, 3), (0, 1))

    @pl.when(mp > 0)
    def _():
        x_halo().wait_recv()

    @pl.when(mp == 0)
    def _():
        xv[0] = jnp.zeros((64, 2048), BF)

    prepare(0)
    convolve(0, acc_x)
    turn_x(0)
    for rh in range(2):
        slope(0, rh, bk[rh])

    lane = lax.broadcasted_iota(jnp.int32, (16, 128), 1)

    @pl.loop(0, 3)
    def _(a):
        acc = acc_a[a] + grad_a_dot(a, (0,))
        for b in range(3):
            this = acc[b * 128 : b * 128 + 128, :128]
            last = acc[b * 128 + 96 : b * 128 + 128, 128:]
            turned = pltpu.roll(this, 64, 1)
            sums = (last + turned[32:64], this[0:32] + turned[64:96], this[32:64] + turned[96:128])
            for c in range(3):
                packed = jnp.where(lane < 64, sums[c][:16], pltpu.roll(sums[c][16:], 64, 1))
                ga_f[pl.ds(pl.multiple_of(a * 144 + b * 48 + c * 16, 16), 16), :] = packed

    ga_f[432:512, :] = jnp.zeros((80, 128), F32)
    ga_s[...] = ga_f[...].reshape(GROUP, ROWS_A, 128).astype(BF)
    others(GROUP, me, lambda i: a1_copy(i, me).start())
    ga_1[me] = ga_s[me]

    turn_h(0)
    grad_b_rows(1, (0, 2), (0, 1))
    gb_f[:, 216:224, :] = jnp.zeros((8, 8, 128), F32)
    gb_s[...] = gb_f[:, pl.ds(pl.multiple_of((1 - core) * HALF, 8), HALF), :].astype(BF)
    b0_copy().start()

    def features_of(plane, terms):
        lhs = [hs[p, b] for p, _ in terms for b in range(3)]
        rhs = [wb[a * 3 + b] for _, a in terms for b in range(3)]
        both = dot(jnp.concatenate(lhs, axis=1), jnp.concatenate(rhs, axis=0))
        out = (both[:, :128] + later(both[:, 128:])).astype(BF)
        turned = dot_tn(out, order[:256]).astype(BF)
        ft[:, :, plane * 256 : plane * 256 + 256] = turned.reshape(8, 16, 256)

    features_of(0, [(0, 1), (1, 2)])
    b0_copy().wait_recv()
    own = pl.ds(pl.multiple_of(core * HALF, 8), HALF)
    gb_h[...] = (gb_f[:, own, :] + gb_0[...].astype(F32)).astype(BF)
    others(SLABS, mp, lambda i: b1_copy(i, mp).start())
    gb_1[mp] = gb_h[mp]
    features_of(1, [(1, 0), (2, 1), (3, 2)])
    features_of(2, [(3, 0)])
    others(SLABS, mp, lambda i: ft_copy(i, mp).start())
    fr[mp] = ft[mp]

    others(GROUP, me, lambda i: a1_copy(i, i).wait_recv())
    ga_2s[...] = jnp.sum(ga_1[...].astype(F32), axis=0)
    others(ring, rank, lambda i: a2_copy(i, rank).start())
    ga_2[rank] = ga_2s[...]

    others(SLABS, mp, lambda i: b1_copy(i, i).wait_recv())
    gb_2s[...] = jnp.sum(gb_1[...].astype(F32), axis=0).astype(BF)
    others(ring, rank, lambda i: b2_copy(i, rank).start())
    gb_2[rank] = gb_2s[...]

    others(ring, rank, lambda i: a2_copy(i, i).wait_recv())
    ga_3s[...] = (jnp.sum(ga_2[...], axis=0) * scale_a).astype(BF)
    others(GROUP, me, lambda i: a3_copy(i, me).start())
    ga_3[me] = ga_3s[...]

    others(ring, rank, lambda i: b2_copy(i, i).wait_recv())
    gb_3[core] = jnp.sum(gb_2[...].astype(F32), axis=0) * scale_b
    b3_copy(core).start()

    others(SLABS, mp, lambda i: ft_copy(i, i).wait_recv())
    for e in range(SLABS):
        first = fr[e, :, 0:256].astype(F32)
        if e > 0:
            first = first + fr[e - 1, :, 512:768].astype(F32)
        planes = jnp.concatenate([first.astype(BF), fr[e, :, 256:512]], axis=1)
        feat[e * 512 : e * 512 + 512, :] = dot_tn(planes, eye).astype(BF)

    @pl.when(mp < SLABS - 1)
    def _():
        x_halo().wait_send()

    others(SLABS, mp, lambda i: kb_copy(i, mp).wait_send())
    kc_copy(core).wait_send()
    others(SLABS, mp, lambda i: ct_copy(i, mp).wait_send())
    others(SLABS, mp, lambda i: ft_copy(i, mp).wait_send())
    b0_copy().wait_send()
    others(SLABS, mp, lambda i: b1_copy(i, mp).wait_send())
    others(ring, rank, lambda i: b2_copy(i, rank).wait_send())
    others(GROUP, me, lambda i: a1_copy(i, me).wait_send())
    others(ring, rank, lambda i: a2_copy(i, rank).wait_send())

    b3_copy(1 - core).wait_recv()
    gb[...] = gb_3[...]
    b3_copy(core).wait_send()
    others(GROUP, me, lambda i: a3_copy(i, me).wait_send())
    others(GROUP, me, lambda i: a3_copy(i, i).wait_recv())
    ga[...] = ga_3[...]


def finish(feat_in, ga_in, gb_in, feat, ga, gb, ga_v, sem):
    rest = 216 - HALF
    moves = [
        (feat_in, feat),
        (gb_in.at[0], gb.at[pl.ds(0, HALF)]),
        (gb_in.at[1, pl.ds(0, rest)], gb.at[pl.ds(HALF, rest)]),
        (ga_v, ga),
    ]
    copies = [pltpu.make_async_copy(src, dst, sem.at[place]) for place, (src, dst) in enumerate(moves)]
    for copy in copies[:-1]:
        copy.start()
    whole = ga_in[...].astype(F32).reshape(GROUP * ROWS_A, 128)[:432].reshape(27, 16, 128)
    ga_v[:, 0:16, :] = whole[:, :, :64]
    ga_v[:, 16:32, :] = whole[:, :, 64:]
    copies[-1].start()
    for copy in copies:
        copy.wait()


def hbm(array):
    return pltpu.with_memory_space_constraint(array, pltpu.HBM)


def shards(ring, samples, volume, kernel_a, kernel_b, cotangent):
    scale_a = 1.0 / math.sqrt(samples * 32**3)
    scale_b = 1.0 / math.sqrt(samples * 16**3)
    vmem = pltpu.VMEM
    dma = pltpu.SemaphoreType.DMA
    scratch = [
        vmem((9, 64, 2048), BF),
        vmem((9, 96, 64), BF),
        vmem((216, 128), BF),
        vmem((4096, 16), BF),
        vmem((9, 5, 256, 128), BF),
        vmem((9, 5, 128, 256), BF),
        vmem((9, 128, 256), BF),
        vmem((4, 2, 256, 128), F32),
        vmem((4, 3, 256, 128), BF),
        vmem((4, 3, 128, 256), BF),
        vmem((16, 4352), BF),
        vmem((8, 16, 768), BF),
        vmem((CORES, HALF, 128), BF),
        vmem((CORES, 8, HALF, 128), BF),
        vmem((8, 224, 128), F32),
        vmem((9, 128, 256), BF),
        vmem((9, 128, 256), BF),
        vmem((3, 2, 256, 128), BF),
        vmem((3, 256, 256), BF),
        vmem((8, 16, 768), BF),
        vmem((8, 16, 768), BF),
        vmem((4, 2, 256, 256), BF),
        vmem((2, 256, 128), F32),
        vmem((3, 384, 256), F32),
        vmem((2, 256, 256), F32),
        vmem((8, 224, 128), F32),
        vmem((8, HALF, 128), BF),
        vmem((8, HALF, 128), BF),
        vmem((8, HALF, 128), BF),
        vmem((8, HALF, 128), BF),
        vmem((HALF, 128), BF),
        vmem((ring, HALF, 128), BF),
        vmem((CORES, HALF, 128), F32),
        vmem((512, 128), F32),
        vmem((GROUP, ROWS_A, 128), BF),
        vmem((GROUP, ROWS_A, 128), BF),
        vmem((ROWS_A, 128), F32),
        vmem((ring, ROWS_A, 128), F32),
        vmem((ROWS_A, 128), BF),
        vmem((GROUP, ROWS_A, 128), BF),
        dma((8,)),
        dma((3,)),
        dma,
        dma,
        dma((8,)),
        dma((8,)),
        dma((8,)),
        dma((8,)),
        dma,
        dma,
        dma((8,)),
        dma((8,)),
        dma,
        dma,
        dma((8,)),
        dma((8,)),
        dma((ring,)),
        dma((ring,)),
        dma,
        dma,
        dma((GROUP,)),
        dma((GROUP,)),
        dma((ring,)),
        dma((ring,)),
        dma((GROUP,)),
        dma((GROUP,)),
    ]
    in_vmem = pl.BlockSpec(memory_space=pltpu.VMEM)
    in_hbm = pl.BlockSpec(memory_space=pltpu.HBM)
    parts = pl.pallas_call(
        functools.partial(body, ring, scale_a, scale_b),
        out_shape=(
            jax.ShapeDtypeStruct((4096, 16), BF),
            jax.ShapeDtypeStruct((GROUP, ROWS_A, 128), BF),
            jax.ShapeDtypeStruct((CORES, HALF, 128), F32),
        ),
        in_specs=[in_hbm] * 4,
        out_specs=(in_vmem,) * 3,
        scratch_shapes=scratch,
        compiler_params=pltpu.CompilerParams(
            collective_id=0, has_side_effects=True, vmem_limit_bytes=48 * 1024 * 1024
        ),
        cost_estimate=pl.CostEstimate(flops=1600000000, bytes_accessed=4000000, transcendentals=0),
    )(
        hbm(volume.reshape(8, 64, 2048)),
        hbm(kernel_a.reshape(9, 96, 64)),
        hbm(kernel_b.reshape(216, 128)),
        hbm(cotangent.reshape(4096, 16)),
    )
    feat, ga, gb = pl.pallas_call(
        finish,
        out_shape=(
            jax.ShapeDtypeStruct((4096, 16), BF),
            jax.ShapeDtypeStruct((27, 32, 64), F32),
            jax.ShapeDtypeStruct((216, 128), F32),
        ),
        in_specs=[in_vmem] * 3,
        out_specs=(in_hbm, in_hbm, in_hbm),
        scratch_shapes=[vmem((27, 32, 64), F32), dma((4,))],
        compiler_params=pltpu.CompilerParams(vmem_limit_bytes=4 * 1024 * 1024),
    )(*parts)
    return (
        feat.reshape(1, 16, 16, 16, 16),
        ga.reshape(3, 3, 3, 32, 64),
        gb.reshape(3, 3, 3, 8, 128),
    )


def solution(mesh):
    ring = mesh.shape["dp"] // CORES
    return jax.shard_map(
        functools.partial(shards, ring, mesh.shape["dp"]),
        mesh=mesh,
        in_specs=(
            P("dp", "mp", None, None),
            P(),
            P(None, None, None, "mp", None),
            P("dp", None, None, None, "mp"),
        ),
        out_specs=(P("dp", None, None, None, "mp"), P(), P(None, None, None, "mp", None)),
        check_vma=False,
    )
```

```python
import functools
import math

import jax
import jax.numpy as jnp
from jax import lax
from jax.experimental import pallas as pl
from jax.experimental.pallas import tpu as pltpu
from jax.sharding import PartitionSpec as P

BF = jnp.bfloat16
F32 = jnp.float32
MESH = pl.DeviceIdType.MESH
SLABS = 8
CORES = 2
GROUP = SLABS * CORES
HALF = 112
ROWS_A = 32


def dot(lhs, rhs):
    return jnp.dot(lhs, rhs, preferred_element_type=F32)


def dot_nt(lhs, rhs):
    return lax.dot_general(lhs, rhs, (((1,), (1,)), ((), ())), preferred_element_type=F32)


def dot_tn(lhs, rhs):
    return lax.dot_general(lhs, rhs, (((0,), (0,)), ((), ())), preferred_element_type=F32)


def later(tiles):
    zero = jnp.zeros((16, tiles.shape[1]), tiles.dtype)
    return jnp.concatenate([zero, tiles[:-16]], axis=0)


def earlier(tiles):
    zero = jnp.zeros((16, tiles.shape[1]), tiles.dtype)
    return jnp.concatenate([tiles[16:], zero], axis=0)


def row_below(tiles):
    rolled = pltpu.roll(tiles.astype(F32), 1, 0)
    row = lax.broadcasted_iota(jnp.int32, tiles.shape, 0)
    return jnp.where(lax.rem(row, 16) == 0, 0.0, rolled).astype(BF)


def body(
    ring,
    scale_a,
    scale_b,
    x,
    ka_hbm,
    kb_hbm,
    cot_hbm,
    feat,
    ga,
    gb,
    xv,
    ka,
    kb,
    cot,
    xs,
    xt,
    wa,
    pf,
    hs,
    ht,
    ct_loc,
    ct_all,
    kb_half,
    kb_all,
    kb_f,
    wb,
    vb,
    cs,
    cc,
    ft,
    fr,
    dd,
    bk,
    acc_a,
    acc_x,
    gb_f,
    gb_s,
    gb_0,
    gb_h,
    gb_1,
    gb_2s,
    gb_2,
    gb_3,
    ga_f,
    ga_s,
    ga_1,
    ga_2s,
    ga_2,
    ga_3s,
    ga_3,
    x_sem,
    in_sem,
    xh_send,
    xh_recv,
    ct_send,
    ct_recv,
    kb_send,
    kb_recv,
    kc_send,
    kc_recv,
    ft_send,
    ft_recv,
    b0_send,
    b0_recv,
    b1_send,
    b1_recv,
    b2_send,
    b2_recv,
    b3_send,
    b3_recv,
    a1_send,
    a1_recv,
    a2_send,
    a2_recv,
    a3_send,
    a3_recv,
):
    mp = lax.axis_index("mp")
    dp = lax.axis_index("dp")
    core = lax.rem(dp, CORES)
    rank = lax.div(dp, CORES)
    me = mp * CORES + core

    def in_group(index):
        return {"mp": lax.div(index, CORES), "dp": rank * CORES + lax.rem(index, CORES)}

    def in_slabs(index):
        return {"mp": index, "dp": dp}

    def in_ring(index):
        return {"mp": mp, "dp": index * CORES + core}

    def others(size, mine, act):
        @pl.loop(1, size)
        def _(step):
            act(lax.rem(mine + step, size))

    def each(size, mine, act):
        for step in range(1, size):
            act(lax.rem(mine + step, size))

    def remote(src, dst, send, recv, device):
        return pltpu.make_async_remote_copy(
            src_ref=src, dst_ref=dst, send_sem=send, recv_sem=recv, device_id=device, device_id_type=MESH
        )

    def plane_copy(plane):
        return pltpu.make_async_copy(x.at[plane], xv.at[plane + 1], x_sem.at[plane])

    in_cot = pltpu.make_async_copy(cot_hbm, cot, in_sem.at[0])
    in_kb = pltpu.make_async_copy(kb_hbm, kb, in_sem.at[1])
    in_ka = pltpu.make_async_copy(ka_hbm, ka, in_sem.at[2])
    in_cot.start()
    in_kb.start()
    in_ka.start()

    @pl.loop(0, 8)
    def _(step):
        plane_copy(7 - step).start()

    barrier = pltpu.get_barrier_semaphore()
    others(GROUP, me, lambda i: pl.semaphore_signal(barrier, inc=1, device_id=in_group(i), device_id_type=MESH))
    others(ring, rank, lambda i: pl.semaphore_signal(barrier, inc=1, device_id=in_ring(i), device_id_type=MESH))

    in_kb.wait()
    in_ka.wait()
    in_cot.wait()

    eye = (
        lax.broadcasted_iota(jnp.int32, (16, 16), 0) == lax.broadcasted_iota(jnp.int32, (16, 16), 1)
    ).astype(BF)

    @pl.loop(0, 8)
    def _(pair):
        rows = cot[pl.ds(pl.multiple_of(pair * 512, 512), 512), :]
        ct_loc[:, pl.ds(pl.multiple_of(pair * 512, 512), 512)] = dot_nt(eye, rows).astype(BF)

    ct_loc[:, 4096:4352] = jnp.zeros((16, 256), BF)
    share = jnp.concatenate([kb[...].astype(F32), jnp.zeros((8, 128), F32)], axis=0).astype(BF)
    kb_half[0] = share[:HALF]
    kb_half[1] = share[HALF:]
    kb_all[core, mp] = kb_half[core]

    @pl.loop(0, 9)
    def _(ab):
        k0 = ka[ab, 0:32, :]
        k1 = ka[ab, 32:64, :]
        k2 = ka[ab, 64:96, :]
        no = jnp.zeros((32, 64), BF)
        wa[ab, 0:32, :] = jnp.concatenate([k1, no, no, no], axis=1)
        wa[ab, 32:64, :] = jnp.concatenate([k2, k0, no, no], axis=1)
        wa[ab, 64:96, :] = jnp.concatenate([no, k1, no, no], axis=1)
        wa[ab, 96:128, :] = jnp.concatenate([no, k2, k0, no], axis=1)

    pick_row = lax.broadcasted_iota(jnp.int32, (80, 64), 0)
    pick_col = lax.broadcasted_iota(jnp.int32, (80, 64), 1)
    pick = (pick_col == 4 * lax.rem(pick_row, 16) + lax.div(pick_row, 16) - 1).astype(BF)

    def prepare(index):
        rows = dot(pick, xv[index]).astype(BF)
        for s in range(5):
            for q in range(16):
                xs[index, s, q * 16 : q * 16 + 16, :] = rows[s * 16 : s * 16 + 16, q * 128 : q * 128 + 128]

    def conv_dot(depth, rh, offsets):
        parts = [xs[2 * depth + a, 2 * rh + b] for a in offsets for b in range(3)]
        weights = wa[3 * offsets[0] : 3 * offsets[-1] + 3].reshape(3 * len(offsets) * 128, 256)
        return dot(jnp.concatenate(parts, axis=1), weights)

    def convolve(depth, begun=None):
        for rh in range(2):
            if begun is None:
                both = conv_dot(depth, rh, (0, 1, 2))
            else:
                both = conv_dot(depth, rh, (0,)) + begun[rh]
            pre = both[:, :128] + later(both[:, 128:])
            pf[depth, rh] = pre
            hidden = jnp.where(pre > 0, pre, 0.3 * pre).astype(BF)
            hs[depth, rh + 1] = hidden
            if rh == 1:
                hs[depth, 0] = row_below(hidden)

    def both_planes(depth):
        plane_copy(2 * depth).wait()
        prepare(2 * depth + 1)
        plane_copy(2 * depth - 1).wait()
        prepare(2 * depth)
        convolve(depth)

    pl.semaphore_wait(barrier, GROUP - 1 + ring - 1)

    def x_halo():
        return remote(x.at[7], xv.at[0], xh_send, xh_recv, in_slabs(mp + 1))

    def ct_copy(peer, slot):
        src = ct_loc.at[:, pl.ds(pl.multiple_of(peer * 512, 512), 768)]
        return remote(src, ct_all.at[slot], ct_send.at[peer], ct_recv.at[slot], in_slabs(peer))

    def kb_copy(peer, slot):
        return remote(
            kb_all.at[core, mp], kb_all.at[core, slot], kb_send.at[peer], kb_recv.at[slot], in_slabs(peer)
        )

    def kc_copy(half):
        return remote(kb_all.at[half], kb_all.at[half], kc_send, kc_recv, in_group(mp * CORES + 1 - core))

    def ft_copy(peer, slot):
        return remote(ft.at[peer], fr.at[slot], ft_send.at[peer], ft_recv.at[slot], in_slabs(peer))

    def b0_copy():
        return remote(gb_s, gb_0, b0_send, b0_recv, in_group(mp * CORES + 1 - core))

    def b1_copy(peer, slot):
        return remote(gb_h.at[peer], gb_1.at[slot], b1_send.at[peer], b1_recv.at[slot], in_slabs(peer))

    def b2_copy(peer, slot):
        return remote(gb_2s, gb_2.at[slot], b2_send.at[peer], b2_recv.at[slot], in_ring(peer))

    def b3_copy(slot):
        return remote(gb_3.at[core], gb_3.at[slot], b3_send, b3_recv, in_group(mp * CORES + 1 - core))

    def a1_copy(peer, slot):
        return remote(ga_s.at[peer], ga_1.at[slot], a1_send.at[peer], a1_recv.at[slot], in_group(peer))

    def a2_copy(peer, slot):
        return remote(ga_2s, ga_2.at[slot], a2_send.at[peer], a2_recv.at[slot], in_ring(peer))

    def a3_copy(peer, slot):
        return remote(ga_3s, ga_3.at[slot], a3_send.at[peer], a3_recv.at[slot], in_group(peer))

    others(SLABS, mp, lambda i: kb_copy(i, mp).start())
    others(SLABS, mp, lambda i: ct_copy(i, mp).start())

    @pl.when(mp < SLABS - 1)
    def _():
        x_halo().start()

    ct_all[mp] = ct_loc[:, pl.ds(pl.multiple_of(mp * 512, 512), 768)]

    plane_copy(7).wait()
    prepare(8)
    both_planes(3)

    @pl.loop(0, 2)
    def _(step):
        both_planes(2 - step)

    plane_copy(0).wait()
    prepare(1)
    for rh in range(2):
        acc_x[rh] = conv_dot(0, rh, (1, 2))

    def turn_x(index):
        for s in range(5):
            xt[index, s] = xs[index, s].T

    def turn_h(index):
        for b in range(3):
            ht[index, b] = hs[index, b].T

    @pl.loop(1, 9)
    def _(index):
        turn_x(index)

    @pl.loop(1, 4)
    def _(index):
        turn_h(index)

    others(SLABS, mp, lambda i: kb_copy(i, i).wait_recv())
    kc_copy(core).start()

    kc_copy(1 - core).wait_recv()

    @pl.loop(0, 8)
    def _(e):
        kb_f[e, 0:HALF] = kb_all[0, e].astype(F32)
        kb_f[e, HALF : 2 * HALF] = kb_all[1, e].astype(F32)

    @pl.loop(0, 9)
    def _(ab):
        k0, k1, k2 = [
            kb_f[:, pl.ds(pl.multiple_of(ab * 24 + c * 8, 8), 8), :].reshape(64, 128) for c in range(3)
        ]
        this = jnp.concatenate([k1, k2], axis=0)
        last = jnp.concatenate([jnp.zeros((64, 128), F32), k0], axis=0)
        wb[ab] = jnp.concatenate([this, last], axis=1).astype(BF)
        vb[ab] = jnp.concatenate([this.T, last.T], axis=1).astype(BF)

    others(SLABS, mp, lambda i: ct_copy(i, i).wait_recv())
    order_row = lax.broadcasted_iota(jnp.int32, (512, 256), 0)
    order_col = lax.broadcasted_iota(jnp.int32, (512, 256), 1)
    order_pos = lax.rem(order_row, 256)
    order = (
        order_col == (lax.rem(order_pos, 16) + lax.div(order_row, 256)) * 16 + lax.div(order_pos, 16)
    ).astype(BF)
    for p in range(3):
        lanes = ct_all[:, :, p * 256 : p * 256 + 256].reshape(128, 256)
        both = dot_nt(order, lanes).astype(BF)
        cs[p, 0] = both[:256]
        cs[p, 1] = both[256:]
        cc[p] = jnp.concatenate([both[:256], earlier(both[:256])], axis=1)

    def slope(depth, rh, back):
        delta = back * jnp.where(pf[depth, rh] > 0, 1.0, 0.3)
        dd[depth, rh] = jnp.concatenate([delta, earlier(delta)], axis=1).astype(BF)

    for depth in range(2):
        for rd in range(2):
            for rh in range(2):
                along = [(1, 0)] if rd == 0 else [(2, 0), (0, 1)]
                down = [(1, 0)] if rh == 0 else [(2, 0), (0, 1)]
                lhs = [cs[depth + ahead, low] for _, ahead in along for _, low in down]
                rhs = [vb[a * 3 + b] for a, _ in along for b, _ in down]
                both = dot(jnp.concatenate(lhs, axis=1), jnp.concatenate(rhs, axis=0))
                back = (both[:, :128] + earlier(both[:, 128:])).astype(BF).astype(F32)
                if depth == 0 and rd == 0:
                    bk[rh] = back
                else:
                    slope(2 * depth + rd, rh, back)

    def grad_a_dot(a, depths):
        lhs = jnp.concatenate(
            [
                jnp.concatenate([xt[2 * depth + a, 2 * rh + b] for b in range(3)], axis=0)
                for depth in depths
                for rh in range(2)
            ],
            axis=1,
        )
        rhs = dd[depths[0] : depths[-1] + 1].reshape(512 * len(depths), 256)
        return dot(lhs, rhs)

    @pl.loop(0, 3)
    def _(a):
        acc_a[a] = grad_a_dot(a, (1, 2, 3))

    def grad_b_rows(a, planes, cots):
        lhs = jnp.concatenate(
            [jnp.concatenate([ht[plane, b] for b in range(3)], axis=0) for plane in planes], axis=1
        )
        rhs = jnp.concatenate([cc[p] for p in cots], axis=0)
        acc = dot(lhs, rhs)
        for b in range(3):
            block = acc[b * 128 : b * 128 + 128]
            pieces = (block[64:, 128:], block[:64, :128], block[64:, :128])
            for c in range(3):
                start = a * 72 + b * 24 + c * 8
                gb_f[:, start : start + 8, :] = pieces[c].reshape(8, 8, 128)

    grad_b_rows(0, (1, 3), (1, 2))
    grad_b_rows(2, (1, 3), (0, 1))

    @pl.when(mp > 0)
    def _():
        x_halo().wait_recv()

    @pl.when(mp == 0)
    def _():
        xv[0] = jnp.zeros((64, 2048), BF)

    prepare(0)
    convolve(0, acc_x)
    turn_x(0)
    for rh in range(2):
        slope(0, rh, bk[rh])

    lane = lax.broadcasted_iota(jnp.int32, (16, 128), 1)

    @pl.loop(0, 3)
    def _(a):
        acc = acc_a[a] + grad_a_dot(a, (0,))
        for b in range(3):
            this = acc[b * 128 : b * 128 + 128, :128]
            last = acc[b * 128 + 96 : b * 128 + 128, 128:]
            turned = pltpu.roll(this, 64, 1)
            sums = (last + turned[32:64], this[0:32] + turned[64:96], this[32:64] + turned[96:128])
            for c in range(3):
                packed = jnp.where(lane < 64, sums[c][:16], pltpu.roll(sums[c][16:], 64, 1))
                ga_f[pl.ds(pl.multiple_of(a * 144 + b * 48 + c * 16, 16), 16), :] = packed

    ga_f[432:512, :] = jnp.zeros((80, 128), F32)
    ga_s[...] = ga_f[...].reshape(GROUP, ROWS_A, 128).astype(BF)
    each(GROUP, me, lambda i: a1_copy(i, me).start())
    ga_1[me] = ga_s[me]

    turn_h(0)
    grad_b_rows(1, (0, 2), (0, 1))
    gb_f[:, 216:224, :] = jnp.zeros((8, 8, 128), F32)
    gb_s[...] = gb_f[:, pl.ds(pl.multiple_of((1 - core) * HALF, 8), HALF), :].astype(BF)
    b0_copy().start()

    def features_of(plane, terms):
        lhs = [hs[p, b] for p, _ in terms for b in range(3)]
        rhs = [wb[a * 3 + b] for _, a in terms for b in range(3)]
        both = dot(jnp.concatenate(lhs, axis=1), jnp.concatenate(rhs, axis=0))
        out = (both[:, :128] + later(both[:, 128:])).astype(BF)
        turned = dot_tn(out, order[:256]).astype(BF)
        ft[:, :, plane * 256 : plane * 256 + 256] = turned.reshape(8, 16, 256)

    features_of(0, [(0, 1), (1, 2)])
    b0_copy().wait_recv()
    own = pl.ds(pl.multiple_of(core * HALF, 8), HALF)
    gb_h[...] = (gb_f[:, own, :] + gb_0[...].astype(F32)).astype(BF)
    each(SLABS, mp, lambda i: b1_copy(i, mp).start())
    gb_1[mp] = gb_h[mp]
    features_of(1, [(1, 0), (2, 1), (3, 2)])
    features_of(2, [(3, 0)])
    others(SLABS, mp, lambda i: ft_copy(i, mp).start())
    fr[mp] = ft[mp]

    others(GROUP, me, lambda i: a1_copy(i, i).wait_recv())
    ga_2s[...] = jnp.sum(ga_1[...].astype(F32), axis=0)
    each(ring, rank, lambda i: a2_copy(i, rank).start())
    ga_2[rank] = ga_2s[...]

    others(SLABS, mp, lambda i: b1_copy(i, i).wait_recv())
    gb_2s[...] = jnp.sum(gb_1[...].astype(F32), axis=0).astype(BF)
    each(ring, rank, lambda i: b2_copy(i, rank).start())
    gb_2[rank] = gb_2s[...]

    others(ring, rank, lambda i: a2_copy(i, i).wait_recv())
    ga_3s[...] = (jnp.sum(ga_2[...], axis=0) * scale_a).astype(BF)
    each(GROUP, me, lambda i: a3_copy(i, me).start())
    ga_3[me] = ga_3s[...]

    others(ring, rank, lambda i: b2_copy(i, i).wait_recv())
    gb_3[core] = jnp.sum(gb_2[...].astype(F32), axis=0) * scale_b
    b3_copy(core).start()

    others(SLABS, mp, lambda i: ft_copy(i, i).wait_recv())
    for e in range(SLABS):
        first = fr[e, :, 0:256].astype(F32)
        if e > 0:
            first = first + fr[e - 1, :, 512:768].astype(F32)
        planes = jnp.concatenate([first.astype(BF), fr[e, :, 256:512]], axis=1)
        feat[e * 512 : e * 512 + 512, :] = dot_tn(planes, eye).astype(BF)

    @pl.when(mp < SLABS - 1)
    def _():
        x_halo().wait_send()

    others(SLABS, mp, lambda i: kb_copy(i, mp).wait_send())
    kc_copy(core).wait_send()
    others(SLABS, mp, lambda i: ct_copy(i, mp).wait_send())
    others(SLABS, mp, lambda i: ft_copy(i, mp).wait_send())
    b0_copy().wait_send()
    others(SLABS, mp, lambda i: b1_copy(i, mp).wait_send())
    others(ring, rank, lambda i: b2_copy(i, rank).wait_send())
    others(GROUP, me, lambda i: a1_copy(i, me).wait_send())
    others(ring, rank, lambda i: a2_copy(i, rank).wait_send())

    b3_copy(1 - core).wait_recv()
    gb[...] = gb_3[...]
    b3_copy(core).wait_send()
    others(GROUP, me, lambda i: a3_copy(i, me).wait_send())
    others(GROUP, me, lambda i: a3_copy(i, i).wait_recv())
    ga[...] = ga_3[...]


def finish(feat_in, ga_in, gb_in, feat, ga, gb, ga_v, sem):
    rest = 216 - HALF
    moves = [
        (feat_in, feat),
        (gb_in.at[0], gb.at[pl.ds(0, HALF)]),
        (gb_in.at[1, pl.ds(0, rest)], gb.at[pl.ds(HALF, rest)]),
        (ga_v, ga),
    ]
    copies = [pltpu.make_async_copy(src, dst, sem.at[place]) for place, (src, dst) in enumerate(moves)]
    for copy in copies[:-1]:
        copy.start()
    whole = ga_in[...].astype(F32).reshape(GROUP * ROWS_A, 128)[:432].reshape(27, 16, 128)
    ga_v[:, 0:16, :] = whole[:, :, :64]
    ga_v[:, 16:32, :] = whole[:, :, 64:]
    copies[-1].start()
    for copy in copies:
        copy.wait()


def hbm(array):
    return pltpu.with_memory_space_constraint(array, pltpu.HBM)


def shards(ring, samples, volume, kernel_a, kernel_b, cotangent):
    scale_a = 1.0 / math.sqrt(samples * 32**3)
    scale_b = 1.0 / math.sqrt(samples * 16**3)
    vmem = pltpu.VMEM
    dma = pltpu.SemaphoreType.DMA
    scratch = [
        vmem((9, 64, 2048), BF),
        vmem((9, 96, 64), BF),
        vmem((216, 128), BF),
        vmem((4096, 16), BF),
        vmem((9, 5, 256, 128), BF),
        vmem((9, 5, 128, 256), BF),
        vmem((9, 128, 256), BF),
        vmem((4, 2, 256, 128), F32),
        vmem((4, 3, 256, 128), BF),
        vmem((4, 3, 128, 256), BF),
        vmem((16, 4352), BF),
        vmem((8, 16, 768), BF),
        vmem((CORES, HALF, 128), BF),
        vmem((CORES, 8, HALF, 128), BF),
        vmem((8, 224, 128), F32),
        vmem((9, 128, 256), BF),
        vmem((9, 128, 256), BF),
        vmem((3, 2, 256, 128), BF),
        vmem((3, 256, 256), BF),
        vmem((8, 16, 768), BF),
        vmem((8, 16, 768), BF),
        vmem((4, 2, 256, 256), BF),
        vmem((2, 256, 128), F32),
        vmem((3, 384, 256), F32),
        vmem((2, 256, 256), F32),
        vmem((8, 224, 128), F32),
        vmem((8, HALF, 128), BF),
        vmem((8, HALF, 128), BF),
        vmem((8, HALF, 128), BF),
        vmem((8, HALF, 128), BF),
        vmem((HALF, 128), BF),
        vmem((ring, HALF, 128), BF),
        vmem((CORES, HALF, 128), F32),
        vmem((512, 128), F32),
        vmem((GROUP, ROWS_A, 128), BF),
        vmem((GROUP, ROWS_A, 128), BF),
        vmem((ROWS_A, 128), F32),
        vmem((ring, ROWS_A, 128), F32),
        vmem((ROWS_A, 128), BF),
        vmem((GROUP, ROWS_A, 128), BF),
        dma((8,)),
        dma((3,)),
        dma,
        dma,
        dma((8,)),
        dma((8,)),
        dma((8,)),
        dma((8,)),
        dma,
        dma,
        dma((8,)),
        dma((8,)),
        dma,
        dma,
        dma((8,)),
        dma((8,)),
        dma((ring,)),
        dma((ring,)),
        dma,
        dma,
        dma((GROUP,)),
        dma((GROUP,)),
        dma((ring,)),
        dma((ring,)),
        dma((GROUP,)),
        dma((GROUP,)),
    ]
    in_vmem = pl.BlockSpec(memory_space=pltpu.VMEM)
    in_hbm = pl.BlockSpec(memory_space=pltpu.HBM)
    parts = pl.pallas_call(
        functools.partial(body, ring, scale_a, scale_b),
        out_shape=(
            jax.ShapeDtypeStruct((4096, 16), BF),
            jax.ShapeDtypeStruct((GROUP, ROWS_A, 128), BF),
            jax.ShapeDtypeStruct((CORES, HALF, 128), F32),
        ),
        in_specs=[in_hbm] * 4,
        out_specs=(in_vmem,) * 3,
        scratch_shapes=scratch,
        compiler_params=pltpu.CompilerParams(
            collective_id=0, has_side_effects=True, vmem_limit_bytes=48 * 1024 * 1024
        ),
        cost_estimate=pl.CostEstimate(flops=1600000000, bytes_accessed=4000000, transcendentals=0),
    )(
        hbm(volume.reshape(8, 64, 2048)),
        hbm(kernel_a.reshape(9, 96, 64)),
        hbm(kernel_b.reshape(216, 128)),
        hbm(cotangent.reshape(4096, 16)),
    )
    feat, ga, gb = pl.pallas_call(
        finish,
        out_shape=(
            jax.ShapeDtypeStruct((4096, 16), BF),
            jax.ShapeDtypeStruct((27, 32, 64), F32),
            jax.ShapeDtypeStruct((216, 128), F32),
        ),
        in_specs=[in_vmem] * 3,
        out_specs=(in_hbm, in_hbm, in_hbm),
        scratch_shapes=[vmem((27, 32, 64), F32), dma((4,))],
        compiler_params=pltpu.CompilerParams(vmem_limit_bytes=4 * 1024 * 1024),
    )(*parts)
    return (
        feat.reshape(1, 16, 16, 16, 16),
        ga.reshape(3, 3, 3, 32, 64),
        gb.reshape(3, 3, 3, 8, 128),
    )


def solution(mesh):
    ring = mesh.shape["dp"] // CORES
    return jax.shard_map(
        functools.partial(shards, ring, mesh.shape["dp"]),
        mesh=mesh,
        in_specs=(
            P("dp", "mp", None, None),
            P(),
            P(None, None, None, "mp", None),
            P("dp", None, None, None, "mp"),
        ),
        out_specs=(P("dp", None, None, None, "mp"), P(), P(None, None, None, "mp", None)),
        check_vma=False,
    )
```
